32 devices in a mesh: space: 8 (over y, x, core), chaos: 4 (over z).
Axes of the slice: x: 2, y: 2, z: 4, core: 2. Of those that a mesh axis runs over, the one named last changes fastest.
Arguments:
- field: bfloat16 [168, 131072], P('chaos', 'space'), may hold values from -6 to 6
- stiffness: bfloat16 [2048, 4096], P(('space', 'chaos')), may hold values from -0.75 to 0.75
- kl_coef: float32 [9, 2048], P(None, ('space', 'chaos')), may hold values from -3 to 3
- triple_mode: int32 [2688], replicated, may hold values from 0 to 7
- triple_row: int32 [2688], replicated, may hold values from 0 to 167
- triple_col: int32 [2688], replicated, may hold values from 0 to 167
- triple_value: float32 [2688], replicated, may hold values from -3 to 3
- die_elem: int32 [4096], P(('space', 'chaos')), may hold values from 0 to 63
- die_side: int32 [4096], P(('space', 'chaos')), may hold values from 0 to 5
- seg_owner: int32 [4096], P(('space', 'chaos')), may hold values from 0 to 31, as said below
- seg_face: int32 [4096], P(('space', 'chaos')), may hold values from 0 to 63
- die_mortar: bfloat16 [4096, 256], P(('space', 'chaos')), may hold values from -1.5 to 1.5
- int_mortar: bfloat16 [4096, 256], P(('space', 'chaos')), may hold values from -1.5 to 1.5
- bump_coef: bfloat16 [4096, 9], P(('space', 'chaos')), may hold values from -3 to 3
- int_elem: int32 [2048], P(('space', 'chaos')), may hold values from 0 to 63
- int_side: int32 [2048], P(('space', 'chaos')), may hold values from 0 to 5
Outputs:
- response: bfloat16 [168, 131072], P('chaos', 'space')
The draws below stay inside these ranges and needn't reach their ends.
Inputs may be any that keep to these rules, and one draw needn't show every extreme that they name: `seg_owner`: in each device's block of 128 segments no owner appears more than 8 times; one owner device receives exactly 8 segments from every device's block.
All inputs are finite; a program needn't handle non-finite values.
Results may differ from the reference program's by a relative error of at most 0.006.
Values may be sent and summed in bfloat16 or wider, within the bound.
A program may use at most 64 MiB of HBM per device.

```python
import jax
import jax.numpy as jnp
import numpy as np
from jax import lax

P_SIZE = 168
MODES = 8
ELEM_NODES = 64
E_DEV = 64
SEG_DEV = 128
IFACE_DEV = 64
CAP = 8
TRIPLES = 2688
NELEM = 2048
NDOF = 131072
SEGS = 4096
IFACES = 2048
DEVICES = 32


def draw_seg_owner(key, part):
    base_key = jax.random.fold_in(key, 11)
    special_key, block_keys = jax.random.split(base_key)
    special = jax.random.randint(special_key, (), 0, DEVICES).astype(jnp.int32)

    def one_block(block_key):
        first_key, second_key = jax.random.split(block_key)
        shuffled = jax.random.permutation(first_key, DEVICES * CAP)
        owners = (shuffled // CAP).astype(jnp.int32)
        ranking = jnp.argsort((owners == special).astype(jnp.int32), stable=True)
        others = owners[ranking][:SEG_DEV - CAP]
        filled = jnp.concatenate([jnp.full((CAP,), special, jnp.int32), others])
        return filled[jax.random.permutation(second_key, SEG_DEV)]
    return jax.vmap(one_block)(jax.random.split(block_keys, DEVICES)).reshape(-1).astype(jnp.int32)


def touch_ends(entries, key, smallest, largest):
    longest = entries.shape.index(max(entries.shape))
    spots = []
    for shift in (0, 1):
        where = [jax.random.randint(jax.random.fold_in(key, axis), (), 0, length) for axis, length in enumerate(entries.shape)]
        where[longest] = (where[longest] + shift) % entries.shape[longest]
        spots.append(tuple(where))
    return entries.at[spots[0]].set(smallest).at[spots[1]].set(largest)


def block_scale(own_key, dims, pieces, least, largest):
    def one(axis_at, blocks):
        steps = jax.random.uniform(jax.random.fold_in(jax.random.fold_in(own_key, 6), axis_at), (blocks,), jnp.float32, least / len(pieces), largest / len(pieces))
        return jnp.repeat(jnp.exp(steps), dims[axis_at] // blocks).reshape((-1,) + (1,) * (len(dims) - axis_at - 1))

    loudness = one(*pieces[0])
    for cut in pieces[1:]:
        loudness = loudness * one(*cut)
    return loudness


def scatter_about(key, shape, width, reach, cuts=(), held_as=jnp.bfloat16):
    values = jax.random.normal(key, shape, jnp.float32) * width
    if len(cuts) > 0:
        values = block_scale(key, shape, cuts, -0.22, 0.18) * values
    return jnp.clip(values, min=-reach, max=reach).astype(held_as)


def setup_inputs(seed: int = 0) -> dict:
    seeds = jax.random.split(jax.random.key(seed), 17)
    field = scatter_about(seeds[0], (P_SIZE, NDOF), 1.0, 6.0, ((0, 4), (1, 8)))
    stiffness = scatter_about(seeds[1], (NELEM, ELEM_NODES * ELEM_NODES), ELEM_NODES ** -0.5, 0.75, ((0, 32),))
    kl_coef = scatter_about(seeds[2], (MODES + 1, NELEM), 0.5, 3.0, ((1, 32),), jnp.float32)
    triple_mode = touch_ends(jax.random.randint(seeds[3], (TRIPLES,), 0, MODES), jax.random.fold_in(seeds[3], 1), 0, MODES - 1).astype(jnp.int32)
    triple_row = touch_ends(jax.random.randint(seeds[4], (TRIPLES,), 0, P_SIZE), jax.random.fold_in(seeds[4], 1), 0, P_SIZE - 1).astype(jnp.int32)
    triple_col = touch_ends(jax.random.randint(seeds[5], (TRIPLES,), 0, P_SIZE), jax.random.fold_in(seeds[5], 1), 0, P_SIZE - 1).astype(jnp.int32)
    triple_value = scatter_about(seeds[6], (TRIPLES,), 0.5, 3.0, (), jnp.float32)
    die_elem = touch_ends(jax.random.randint(seeds[7], (SEGS,), 0, E_DEV), jax.random.fold_in(seeds[7], 1), 0, E_DEV - 1).astype(jnp.int32)
    die_side = touch_ends(jax.random.randint(seeds[8], (SEGS,), 0, 6), jax.random.fold_in(seeds[8], 1), 0, 5).astype(jnp.int32)
    seg_owner = draw_seg_owner(jax.random.fold_in(seeds[16], 71), 0)
    seg_face = touch_ends(jax.random.randint(seeds[10], (SEGS,), 0, IFACE_DEV), jax.random.fold_in(seeds[10], 1), 0, IFACE_DEV - 1).astype(jnp.int32)
    die_mortar = scatter_about(seeds[11], (SEGS, 256), 16 ** -0.5, 1.5, ((0, 32),))
    int_mortar = scatter_about(seeds[12], (SEGS, 256), 16 ** -0.5, 1.5, ((0, 32),))
    bump_coef = scatter_about(seeds[13], (SEGS, MODES + 1), 0.5, 3.0, ((0, 32),))
    int_elem = touch_ends(jax.random.randint(seeds[14], (IFACES,), 0, E_DEV), jax.random.fold_in(seeds[14], 1), 0, E_DEV - 1).astype(jnp.int32)
    int_side = touch_ends(jax.random.randint(seeds[15], (IFACES,), 0, 6), jax.random.fold_in(seeds[15], 1), 0, 5).astype(jnp.int32)
    return {"field": field, "stiffness": stiffness, "kl_coef": kl_coef, "triple_mode": triple_mode, "triple_row": triple_row, "triple_col": triple_col, "triple_value": triple_value, "die_elem": die_elem, "die_side": die_side, "seg_owner": seg_owner, "seg_face": seg_face, "die_mortar": die_mortar, "int_mortar": int_mortar, "bump_coef": bump_coef, "int_elem": int_elem, "int_side": int_side}


def face_nodes():
    node_rows = []
    for side_idx in range(6):
        normal_axis = side_idx // 2
        plane_level = 3 * (side_idx % 2)
        row_nodes = []
        for first_coord in range(4):
            for second_coord in range(4):
                position = [first_coord, second_coord]
                position.insert(normal_axis, plane_level)
                row_nodes.append(16 * position[0] + 4 * position[1] + position[2])
        node_rows.append(row_nodes)
    return np.array(node_rows, dtype=np.int32)


def reference(field, stiffness, kl_coef, triple_mode, triple_row, triple_col, triple_value, die_elem, die_side, seg_owner, seg_face, die_mortar, int_mortar, bump_coef, int_elem, int_side):
    coupling = jnp.zeros((MODES, P_SIZE, P_SIZE), jnp.float32).at[triple_mode, triple_row, triple_col].add(triple_value).astype(jnp.bfloat16)
    node_table = jnp.asarray(face_nodes())
    kl_nodes = jnp.repeat(kl_coef, ELEM_NODES, axis=1)
    mixed = kl_nodes[0] * field.astype(jnp.float32)
    for mode_idx in range(MODES):
        mixed = mixed + kl_nodes[mode_idx + 1] * jnp.dot(coupling[mode_idx], field, preferred_element_type=jnp.float32)
    mixed = lax.optimization_barrier(mixed.astype(jnp.bfloat16))
    blocks = stiffness.astype(jnp.float32).reshape(NELEM, ELEM_NODES, ELEM_NODES)
    local_out = jnp.einsum("eab,peb->pea", blocks, mixed.astype(jnp.float32).reshape(P_SIZE, NELEM, ELEM_NODES)).reshape(P_SIZE, NDOF)

    seg_index = jnp.arange(SEGS, dtype=jnp.int32)
    die_global = E_DEV * (seg_index // SEG_DEV) + die_elem
    die_nodes = (die_global[:, None] * ELEM_NODES + node_table[die_side]).astype(jnp.int32)
    face_global = (IFACE_DEV * seg_owner + seg_face).astype(jnp.int32)
    int_global = E_DEV * seg_owner + int_elem[face_global]
    int_nodes = (int_global[:, None] * ELEM_NODES + node_table[int_side[face_global]]).astype(jnp.int32)

    die_mats = die_mortar.astype(jnp.float32).reshape(SEGS, 16, 16)
    int_mats = int_mortar.astype(jnp.float32).reshape(SEGS, 16, 16)
    die_face = field[:, die_nodes].astype(jnp.float32)
    die_proj = lax.optimization_barrier(jnp.einsum("sgf,psf->sgp", die_mats, die_face).astype(jnp.bfloat16))
    int_face = field[:, int_nodes].astype(jnp.float32)
    int_proj = jnp.einsum("sgf,psf->sgp", int_mats, int_face)
    jump_vals = lax.optimization_barrier((die_proj.astype(jnp.float32) - int_proj).astype(jnp.bfloat16))

    weights = bump_coef.astype(jnp.float32)
    accum = weights[:, 0][:, None, None] * jump_vals.astype(jnp.float32)
    flat_jump = jump_vals.reshape(SEGS * 16, P_SIZE)
    for mode_idx in range(MODES):
        term = jnp.dot(flat_jump, coupling[mode_idx].T, preferred_element_type=jnp.float32).reshape(SEGS, 16, P_SIZE)
        accum = accum + weights[:, mode_idx + 1][:, None, None] * term
    seg_flux = lax.optimization_barrier(accum.astype(jnp.bfloat16)).astype(jnp.float32)

    die_back = jnp.einsum("sgf,sgp->psf", die_mats, seg_flux).reshape(P_SIZE, SEGS * 16)
    int_back = jnp.einsum("sgf,sgp->psf", int_mats, seg_flux).reshape(P_SIZE, SEGS * 16)
    result = local_out.at[:, die_nodes.reshape(-1)].add(die_back)
    result = result.at[:, int_nodes.reshape(-1)].add(-int_back)
    return result.astype(jnp.bfloat16)
```

```python
import functools

import jax
import jax.numpy as jnp
import numpy as np
from jax import lax
from jax.experimental import pallas as pl
from jax.experimental.pallas import tpu as pltpu
from jax.sharding import PartitionSpec as P

ELEM_NODES = 64
LANES = 128
FACE = 16
VMEM_LIMIT = 56 * 1024 * 1024
NT = (((1,), (1,)), ((), ()))
NN = (((1,), (0,)), ((), ()))
MESH = pl.DeviceIdType.MESH


def face_nodes():
    node_rows = []
    for side_idx in range(6):
        normal_axis = side_idx // 2
        plane_level = 3 * (side_idx % 2)
        row_nodes = []
        for first_coord in range(4):
            for second_coord in range(4):
                position = [first_coord, second_coord]
                position.insert(normal_axis, plane_level)
                row_nodes.append(16 * position[0] + 4 * position[1] + position[2])
        node_rows.append(row_nodes)
    return np.array(node_rows, dtype=np.int32)


def face_select():
    table = np.zeros((LANES, 2 * LANES), np.float32)
    for side, row in enumerate(face_nodes()):
        for point, node in enumerate(row):
            for half in range(2):
                table[half * ELEM_NODES + node, half * LANES + side * FACE + point] = 1.0
    return jnp.asarray(table, jnp.bfloat16)


def mm(a, b, dims=NN):
    return lax.dot_general(a, b, dims, preferred_element_type=jnp.float32)


def iota(shape, dim):
    return lax.broadcasted_iota(jnp.int32, shape, dim)


def hot(mask):
    return jnp.where(mask, 1.0, 0.0).astype(jnp.bfloat16)


def block_diag(flat):
    spread = mm(hot(iota((LANES, 8), 0) // FACE == iota((LANES, 8), 1)), flat)
    own_row = iota((LANES, 256), 1) // FACE == iota((LANES, 256), 0) % FACE
    spread = jnp.where(own_row, spread, 0.0).astype(jnp.bfloat16)
    fold = hot(iota((256, LANES), 0) % FACE == iota((256, LANES), 1) % FACE)
    tiled = mm(spread, fold)
    same = iota((LANES, LANES), 0) // FACE == iota((LANES, LANES), 1) // FACE
    return jnp.where(same, tiled, 0.0).astype(jnp.bfloat16)


def split_rows(part):
    high = part // 16 * 16
    return high, part - high, high + 16


def swap(x):
    row, group = iota(x.shape, 1), iota(x.shape, 2) // FACE
    for k in (1, 2, 4):
        row_bit, group_bit = row // k % 2, group // k % 2
        moved = pltpu.roll(pltpu.roll(x, 8 - k, 1), FACE * k, 2)
        if k < 4:
            other = pltpu.roll(pltpu.roll(x, k, 1), LANES - FACE * k, 2)
            moved = jnp.where(row_bit < group_bit, moved, other)
        x = jnp.where(row_bit == group_bit, x, moved)
    return x


def to_rows(tiles):
    turned = [swap(t.reshape(-1, 8, LANES)) for t in tiles]
    return jnp.concatenate(
        [jnp.concatenate([t[a] for t in turned], axis=0) for a in range(turned[0].shape[0])], axis=1
    ).astype(jnp.bfloat16)


def to_tiles(rows):
    tiles = []
    for h in range(2):
        own = rows[8 * h:8 * h + 8]
        stack = jnp.stack([own[:, a * LANES:(a + 1) * LANES] for a in range(rows.shape[1] // LANES)], axis=0)
        tiles.append(swap(stack).reshape(-1, LANES))
    return tiles


def column(row):
    size = row.shape[1]
    eye = iota((size, size), 0) == iota((size, size), 1)
    return jnp.sum(jnp.where(eye, row, 0), axis=1, keepdims=True)


def split_rows(part):
    high = part // 16 * 16
    return high, part - high, high + 16


def greet(axes):
    barrier = pltpu.get_barrier_semaphore()
    for axis, count in axes:
        me = lax.axis_index(axis)
        for d in range(1, count):
            pl.semaphore_signal(barrier, 1, device_id={axis: lax.rem(me + d, count)}, device_id_type=MESH)


def meet(axes):
    pl.semaphore_wait(pltpu.get_barrier_semaphore(), sum(count - 1 for _, count in axes))


def send(src, dst, sems, d, axis, peer):
    copy = pltpu.make_async_remote_copy(
        src_ref=src, dst_ref=dst, send_sem=sems.at[0, d - 1], recv_sem=sems.at[1, d - 1],
        device_id={axis: peer}, device_id_type=MESH)
    copy.start()
    return copy


def finish(copies):
    for copy in copies:
        copy.wait()


def pack(load, store, tail_ref, part, width):
    high, low, _ = split_rows(part)
    for q in range(16):
        upper, lower = load(q)
        store(slice(q * high, (q + 1) * high), upper)
        tail_ref[q * low:(q + 1) * low, :] = lower.astype(jnp.float32)
    store(slice(16 * high, 16 * part), tail_ref[...].astype(jnp.bfloat16))


def mix(coupling_ref, block, weights):
    total = weights[0:1] * block.astype(jnp.float32)
    for k in range(coupling_ref.shape[0]):
        total = total + weights[k + 1:k + 2] * mm(coupling_ref[k], block)
    return total.astype(jnp.bfloat16)


def slot_ids(requests, n, cap, faces):
    lane = iota((1, LANES), 1)
    return lax.rem(lane // cap, n) * faces + requests


def head_kernel(
    field_ref, stiff_ref, kl_ref, triple_ref, value_ref, index_ref, die_ref, int_ref, sel_ref,
    coupling_out, out_ref, proj_out, int_out, share_out, ask_out, die_diag, int_diag,
    msg, rows, sent, wide, block_ref, faces_ref, table_ref, slots, recv, picked, fp, stiff, die_faces, tail_ref,
    share_sem, ask_sem, field_sem, slot_sem, pick_sem, *, n, ns, cap, faces,
):
    f32, bf16 = jnp.float32, jnp.bfloat16
    me_c, me_s = lax.axis_index("chaos"), lax.axis_index("space")
    axes = (("chaos", n), ("space", ns))
    greet(axes)
    part, local_nodes = field_ref.shape
    nodes = local_nodes // n
    width = nodes // 16
    per = width // LANES
    high, low, pad = split_rows(part)
    wide_lanes = pad * FACE
    modes, all_rows, _ = coupling_out.shape
    sel = sel_ref[...]

    index = index_ref[...]
    owner, seg_face = index[0:1], index[1:2]
    segs = owner.shape[1]
    r, c = iota((segs, segs), 0), iota((segs, segs), 1)
    owner_col, face_col = column(owner), column(seg_face)
    same = owner_col == owner
    rank_row = jnp.sum(jnp.where(same & (r < c), 1, 0), axis=0, keepdims=True)
    rank_col = jnp.sum(jnp.where(same & (c < r), 1, 0), axis=1, keepdims=True)
    base = me_c * (n * cap)
    lane_row = base + lax.rem(owner, n) * cap + rank_row
    lane_col = base + lax.rem(owner_col, n) * cap + rank_col
    left = hot(iota((16, segs), 0) == lax.div(owner, n))
    request = mm(left, jnp.where(c == lane_col, face_col, 0).astype(f32).astype(bf16))
    msg[...] = jnp.zeros(msg.shape, jnp.int32)
    msg[:ns, :] = request[:ns].astype(jnp.int32)
    msg[ns:ns + 1, :] = lax.div(owner, n) * LANES + lane_row
    msg[ns + 1:ns + 2, :] = index[2:3]
    meet(axes)
    share_out[me_c] = msg[...]
    copies = []
    for d in range(1, n):
        copies.append(send(msg, share_out.at[me_c], share_sem, d, "chaos", lax.rem(me_c + d, n)))

    field_copies = []
    for d in range(1, n + 1):
        peer = lax.rem(me_c + d, n)
        start = peer * nodes

        def load(q):
            cols = pl.ds(pl.multiple_of(start + q * width, LANES), width)
            return field_ref[:high, cols], field_ref[high:part, cols]

        def store(where, value):
            if d < n:
                sent[peer, where, :] = value
            else:
                wide[me_c, where, :] = value

        pack(load, store, tail_ref, part, width)
        if d < n:
            field_copies.append(send(sent.at[peer], wide.at[me_c], field_sem, d, "chaos", peer))
    finish(copies)

    total = share_out[0, :ns, :]
    for i in range(1, n):
        total = total + share_out[i, :ns, :]
    for s in range(ns):
        rows[s] = jnp.broadcast_to(total[s:s + 1, :], (8, LANES))
    ask_out[me_s] = rows[me_s]
    copies = []
    for d in range(1, ns):
        peer = lax.rem(me_s + d, ns)
        copies.append(send(rows.at[peer], ask_out.at[me_s], ask_sem, d, "space", peer))

    block_ref[...] = jnp.zeros(block_ref.shape, bf16)
    pairs = nodes // LANES
    step_pairs = block_ref.shape[0]

    def face_step(p, carry):
        for u in range(step_pairs):
            at = p * step_pairs + u
            block_ref[u, :part, :] = field_ref[:, pl.ds(pl.multiple_of(at * LANES, LANES), LANES)]
            found = mm(block_ref[u], sel)
            faces_ref[pl.ds(pl.multiple_of(at * 16, 16), 16), :] = to_rows([found[:, :LANES], found[:, LANES:]])
        return carry

    lax.fori_loop(0, n * pairs // step_pairs, face_step, 0)
    elem_rows = pairs * 16
    for i in range(n):
        code = column(share_out[i, ns + 1:ns + 2, :])
        pick = hot(iota((LANES, elem_rows), 1) == code)
        found = mm(pick[:faces], faces_ref[i * elem_rows:(i + 1) * elem_rows, :])
        table_ref[i * faces:(i + 1) * faces, :] = found.astype(bf16)
    finish(copies)

    slot_copies = []
    for d in range(1, ns + 1):
        peer = lax.rem(me_s + d, ns)
        ids = column(slot_ids(ask_out[peer, 0:1, :], n, cap, faces))
        found = mm(hot(iota((LANES, n * faces), 1) == ids), table_ref[...]).astype(bf16)
        if d < ns:
            slots[peer] = found
            slot_copies.append(send(slots.at[peer], recv.at[me_s], slot_sem, d, "space", peer))
        else:
            recv[me_s] = found

    groups = die_diag.shape[0]

    def diag_step(g, carry):
        die_diag[g] = block_diag(die_ref[g])
        int_diag[g] = block_diag(int_ref[g])
        return carry

    lax.fori_loop(0, groups, diag_step, 0)

    triples = triple_ref[...]
    value = value_ref[...]
    key, col = triples[0:1], triples[1:2]
    coarse = value.astype(bf16).astype(f32)
    at_col = iota((all_rows, key.shape[1]), 0) == col
    right = jnp.concatenate(
        [jnp.where(at_col, coarse, 0.0).astype(bf16), jnp.where(at_col, value - coarse, 0.0).astype(bf16)], axis=0
    )

    def mode_step(k, carry):
        at_row = hot(iota((all_rows, key.shape[1]), 0) + k * all_rows == key)
        both = mm(at_row, right, NT)
        coupling_out[k] = (both[:, :all_rows] + both[:, all_rows:]).astype(bf16)
        return carry

    lax.fori_loop(0, modes, mode_step, 0)

    elems = stiff_ref.shape[0]
    for t in range(ELEM_NODES // 2):
        block = stiff_ref[:, t * LANES:(t + 1) * LANES].astype(f32)
        stiff[pl.ds(2 * t, elems, stride=ELEM_NODES), :] = block
        stiff[pl.ds(2 * t + 1, elems, stride=ELEM_NODES), :] = pltpu.roll(block, ELEM_NODES, 1)

    finish(slot_copies)
    pick_copies = []
    everything = recv[...].reshape(ns * LANES, wide_lanes)
    for d in range(1, n + 1):
        peer = lax.rem(me_c + d, n)
        spot = column(share_out[peer, ns:ns + 1, :])
        found = mm(hot(iota((segs, ns * LANES), 1) == spot), everything).astype(bf16)
        if d < n:
            picked[peer] = found
            pick_copies.append(send(picked.at[peer], int_out.at[me_c], pick_sem, d, "chaos", peer))
        else:
            int_out[me_c] = found

    finish(field_copies)
    keep = iota((16, width), 0) < low
    for i in range(n):
        tail_ref[...] = wide[i, 16 * high:, :].astype(f32)
        for q in range(16):
            first = min(q * low, 16 * low - 16)
            tail = tail_ref[first:first + 16, :]
            if first < q * low:
                tail = pltpu.roll(tail, 16 - (q * low - first), 0)
            tail = jnp.where(keep, tail, 0.0).astype(bf16)
            for h in range(per):
                cols = slice(h * LANES, (h + 1) * LANES)
                fp[q * per + h, i * pad:i * pad + high, :] = wide[i, q * high:(q + 1) * high, cols]
                fp[q * per + h, i * pad + high:(i + 1) * pad, :] = tail[:, cols]

    lower = iota((ELEM_NODES, LANES), 1) < ELEM_NODES

    def element_step(p, carry):
        block = jnp.concatenate([fp[2 * p], fp[2 * p + 1]], axis=1)
        spread = jnp.where(iota((elems, 256), 1) // ELEM_NODES + 4 * p == iota((elems, 256), 0), 1.0, 0.0)
        weights = lax.dot_general(
            kl_ref[...], spread, NN, precision=lax.Precision.HIGHEST, preferred_element_type=f32)
        mixed = mix(coupling_out, block, weights)
        for h in range(2):
            at = pl.multiple_of((2 * p + h) * LANES, LANES)
            even = jnp.where(lower, stiff[pl.ds(at, ELEM_NODES), :], 0.0)
            odd = pltpu.roll(stiff[pl.ds(at + ELEM_NODES, ELEM_NODES), :], ELEM_NODES, 1)
            odd = jnp.where(lower, 0.0, odd)
            diag = jnp.concatenate([even, odd], axis=0).astype(bf16)
            out_ref[2 * p + h] = mm(mixed[:, h * LANES:(h + 1) * LANES], diag, NT)
        return carry

    lax.fori_loop(0, pairs // 2, element_step, 0)

    def die_step(p, carry):
        found = mm(fp[p], sel)
        at = pl.ds(pl.multiple_of(p * 16, 16), 16)
        for i in range(n):
            own = found[i * pad:(i + 1) * pad]
            die_faces[i, at, :] = to_rows([own[:, :LANES], own[:, LANES:]])
        return carry

    lax.fori_loop(0, pairs, die_step, 0)
    code = column(index[3:4])
    pick = hot(iota((segs, elem_rows), 1) == code)
    for i in range(n):
        found = mm(pick, die_faces[i])
        for g in range(groups // 2):
            tiles = to_tiles(found[16 * g:16 * g + 16])
            for h in range(2):
                proj_out[2 * g + h, i * pad:(i + 1) * pad, :] = tiles[h].astype(bf16)

    def project_step(g, carry):
        proj_out[g] = mm(proj_out[g], die_diag[g], NT).astype(bf16)
        return carry

    lax.fori_loop(0, groups, project_step, 0)
    finish(pick_copies)


def tail_kernel(
    faces_ref, proj_ref, die_diag, int_diag, coupling_ref, coef_ref, local_ref, index_ref, share_ref, ask_ref, sel_ref,
    returned, delta_out,
    back_send, back_recv, die_back, out_send, slots, recv, tail_ref,
    back_sem, out_sem, slot_sem, *, n, ns, cap, faces, part,
):
    f32, bf16 = jnp.float32, jnp.bfloat16
    me_c, me_s = lax.axis_index("chaos"), lax.axis_index("space")
    axes = (("chaos", n), ("space", ns))
    greet(axes)
    groups, all_rows, _ = proj_ref.shape
    pairs = local_ref.shape[0]
    high, low, pad = split_rows(part)
    wide_lanes = pad * FACE
    width = returned.shape[2]
    per = width // LANES
    segs = index_ref.shape[1]
    sel = sel_ref[...]

    def flux_step(p, carry):
        at = pl.ds(pl.multiple_of(p * 16, 16), 16)
        tiles = [to_tiles(faces_ref[i, at, :].astype(f32)) for i in range(n)]
        jumps = []
        for h in range(2):
            face = jnp.concatenate([t[h] for t in tiles], axis=0).astype(bf16)
            own = mm(face, int_diag[2 * p + h], NT)
            jumps.append((proj_ref[2 * p + h].astype(f32) - own).astype(bf16))
        spread = hot(iota((segs, 256), 1) // FACE + 16 * p == iota((segs, 256), 0))
        weights = mm(coef_ref[...], spread)
        flux = mix(coupling_ref, jnp.concatenate(jumps, axis=1), weights)
        halves = [flux[:, h * LANES:(h + 1) * LANES] for h in range(2)]
        int_side = [mm(halves[h], int_diag[2 * p + h]) for h in range(2)]
        die_side = [mm(halves[h], die_diag[2 * p + h]) for h in range(2)]
        for i in range(n):
            rows = slice(i * pad, (i + 1) * pad)
            back_send[i, at, :] = to_rows([x[rows] for x in int_side])
            die_back[i, at, :] = to_rows([x[rows] for x in die_side])
        return carry

    lax.fori_loop(0, groups // 2, flux_step, 0)
    meet(axes)
    back_copies = []
    for d in range(1, n):
        peer = lax.rem(me_c + d, n)
        back_copies.append(send(back_send.at[peer], back_recv.at[me_c], back_sem, d, "chaos", peer))
    back_recv[me_c] = back_send[me_c]

    elem_rows = pairs * 16
    place = hot(iota((elem_rows, segs), 0) == index_ref[3:4, :])
    out_copies = []
    for d in range(1, n + 1):
        peer = lax.rem(me_c + d, n)
        found = mm(place, die_back[peer])

        def load(q):
            upper, lower = [], []
            for h in range(per):
                p = q * per + h
                tiles = to_tiles(found[16 * p:16 * p + 16])
                both = jnp.concatenate(tiles, axis=1).astype(bf16)
                own = local_ref[p, pl.ds(pl.multiple_of(peer * pad, 16), pad), :] + mm(both, sel, NT)
                upper.append(own[:high])
                lower.append(own[high:part])
            return jnp.concatenate(upper, axis=1).astype(bf16), jnp.concatenate(lower, axis=1)

        def store(where, value):
            if d < n:
                out_send[peer, where, :] = value
            else:
                returned[me_c, where, :] = value

        pack(load, store, tail_ref, part, width)
        if d < n:
            out_copies.append(send(out_send.at[peer], returned.at[me_c], out_sem, d, "chaos", peer))

    finish(back_copies)
    everything = back_recv[...].reshape(n * segs, wide_lanes)
    spots = jnp.concatenate([share_ref[i, ns:ns + 1, :] for i in range(n)], axis=1)
    slot_copies = []
    for d in range(1, ns + 1):
        peer = lax.rem(me_s + d, ns)
        found = mm(hot(iota((LANES, n * segs), 0) + peer * LANES == spots), everything).astype(bf16)
        if d < ns:
            slots[peer] = found
            slot_copies.append(send(slots.at[peer], recv.at[me_s], slot_sem, d, "space", peer))
        else:
            recv[me_s] = found
    finish(slot_copies)

    ids = jnp.concatenate([slot_ids(ask_ref[s, 0:1, :], n, cap, faces) for s in range(ns)], axis=1)
    everything = recv[...].reshape(ns * LANES, wide_lanes)
    summed = mm(hot(iota((n * faces, ns * LANES), 0) == ids), everything).astype(bf16)
    for i in range(n):
        code = share_ref[i, ns + 1:ns + 2, :][:, :faces]
        found = mm(hot(iota((elem_rows, faces), 0) == code), summed[i * faces:(i + 1) * faces])
        for p in range(pairs):
            both = jnp.concatenate(to_tiles(found[16 * p:16 * p + 16]), axis=1).astype(bf16)
            delta_out[i * pairs + p] = mm(both, sel, NT)
    finish(out_copies)


def receive_kernel(in_ref, delta_ref, out_ref, tail_ref):
    part, nodes = out_ref.shape
    high, low, _ = split_rows(part)
    width = nodes // 16
    per = width // LANES
    tail_ref[...] = in_ref[0, 16 * high:, :].astype(jnp.float32)
    for q in range(16):
        for h in range(per):
            cols = slice(q * width + h * LANES, q * width + (h + 1) * LANES)
            own = slice(h * LANES, (h + 1) * LANES)
            delta = delta_ref[q * per + h]
            upper = in_ref[0, q * high:(q + 1) * high, own].astype(jnp.float32)
            out_ref[:high, cols] = (upper - delta[:high]).astype(jnp.bfloat16)
            lower = tail_ref[q * low:(q + 1) * low, own]
            out_ref[high:part, cols] = (lower - delta[high:part]).astype(jnp.bfloat16)


def call(kernel, outs, args, scratch, collective_id):
    moved = sum(x.size * x.dtype.itemsize for x in (*args, *outs))
    return pl.pallas_call(
        kernel,
        out_shape=outs,
        in_specs=[pl.BlockSpec(memory_space=pltpu.VMEM)] * len(args),
        out_specs=tuple(pl.BlockSpec(memory_space=pltpu.VMEM) for _ in outs),
        scratch_shapes=scratch,
        compiler_params=pltpu.CompilerParams(
            collective_id=collective_id, has_side_effects=True, vmem_limit_bytes=VMEM_LIMIT
        ),
        cost_estimate=pl.CostEstimate(flops=0, bytes_accessed=moved, transcendentals=0),
    )(*args)


def local(
    field,
    stiffness,
    kl_coef,
    triple_mode,
    triple_row,
    triple_col,
    triple_value,
    die_elem,
    die_side,
    seg_owner,
    seg_face,
    die_mortar,
    int_mortar,
    bump_coef,
    int_elem,
    int_side,
):
    n, ns = lax.axis_size("chaos"), lax.axis_size("space")
    part, local_nodes = field.shape
    nodes = local_nodes // n
    segs = die_elem.shape[0]
    cap = max(2, 2 * segs // (n * ns))
    faces = int_elem.shape[0]
    pairs = nodes // LANES
    modes = bump_coef.shape[1] - 1
    high, low, pad = split_rows(part)
    rows = n * pad
    lanes = pad * FACE
    groups = segs // 8
    width = nodes // 16
    bf16, f32, i32 = jnp.bfloat16, jnp.float32, jnp.int32
    sel = face_select()

    index = jnp.stack([
        seg_owner, seg_face, jnp.pad(int_elem * 8 + int_side, (0, segs - faces)), die_elem * 8 + die_side,
    ])
    triples = jnp.stack([
        triple_mode * rows + triple_row // part * pad + triple_row % part, triple_col // part * pad + triple_col % part,
    ])
    height = (ns + 2 + 7) // 8 * 8
    packed = (n, 16 * part, width)

    def sems(count):
        return pltpu.SemaphoreType.DMA((2, count - 1))

    coupling, local_out, proj, int_faces, shared, asked, die_diag, int_diag = call(
        functools.partial(head_kernel, n=n, ns=ns, cap=cap, faces=faces),
        (
            jax.ShapeDtypeStruct((modes, rows, rows), bf16),
            jax.ShapeDtypeStruct((pairs, rows, LANES), f32),
            jax.ShapeDtypeStruct((groups, rows, LANES), bf16),
            jax.ShapeDtypeStruct((n, segs, lanes), bf16),
            jax.ShapeDtypeStruct((n, height, LANES), i32),
            jax.ShapeDtypeStruct((ns, 8, LANES), i32),
            jax.ShapeDtypeStruct((groups, LANES, LANES), bf16),
            jax.ShapeDtypeStruct((groups, LANES, LANES), bf16),
        ),
        (
            field, stiffness, kl_coef, triples, triple_value.reshape(1, -1), index,
            die_mortar.reshape(groups, 8, 256), int_mortar.reshape(groups, 8, 256), sel,
        ),
        (
            pltpu.VMEM((height, LANES), i32),
            pltpu.VMEM((ns, 8, LANES), i32),
            pltpu.VMEM(packed, bf16),
            pltpu.VMEM(packed, bf16),
            pltpu.VMEM((4, pad, LANES), bf16),
            pltpu.VMEM((n * pairs * 16, lanes), bf16),
            pltpu.VMEM((n * faces, lanes), bf16),
            pltpu.VMEM((ns, LANES, lanes), bf16),
            pltpu.VMEM((ns, LANES, lanes), bf16),
            pltpu.VMEM((n, segs, lanes), bf16),
            pltpu.VMEM((pairs, rows, LANES), bf16),
            pltpu.VMEM((2 * pairs * ELEM_NODES, LANES), f32),
            pltpu.VMEM((n, pairs * 16, lanes), bf16),
            pltpu.VMEM((16 * low, width), f32),
            sems(n), sems(ns), sems(n), sems(ns), sems(n),
        ),
        0,
    )
    returned, delta = call(
        functools.partial(tail_kernel, n=n, ns=ns, cap=cap, faces=faces, part=part),
        (
            jax.ShapeDtypeStruct(packed, bf16),
            jax.ShapeDtypeStruct((n * pairs, pad, LANES), f32),
        ),
        (int_faces, proj, die_diag, int_diag, coupling, bump_coef.T, local_out, index, shared, asked, sel),
        (
            pltpu.VMEM((n, segs, lanes), bf16),
            pltpu.VMEM((n, segs, lanes), bf16),
            pltpu.VMEM((n, segs, lanes), bf16),
            pltpu.VMEM(packed, bf16),
            pltpu.VMEM((ns, LANES, lanes), bf16),
            pltpu.VMEM((ns, LANES, lanes), bf16),
            pltpu.VMEM((16 * low, width), f32),
            sems(n), sems(n), sems(ns),
        ),
        1,
    )
    return pl.pallas_call(
        receive_kernel,
        out_shape=jax.ShapeDtypeStruct((part, local_nodes), bf16),
        grid=(n,),
        in_specs=[
            pl.BlockSpec((1, 16 * part, width), lambda c: (c, 0, 0)),
            pl.BlockSpec((pairs, pad, LANES), lambda c: (c, 0, 0)),
        ],
        out_specs=pl.BlockSpec((part, nodes), lambda c: (0, c)),
        scratch_shapes=[pltpu.VMEM((16 * low, width), f32)],
    )(returned, delta)


def solution(mesh):
    in_specs = (
        P("chaos", "space"),
        P(("space", "chaos"), None),
        P(None, ("space", "chaos")),
        P(),
        P(),
        P(),
        P(),
        P(("space", "chaos")),
        P(("space", "chaos")),
        P(("space", "chaos")),
        P(("space", "chaos")),
        P(("space", "chaos"), None),
        P(("space", "chaos"), None),
        P(("space", "chaos"), None),
        P(("space", "chaos")),
        P(("space", "chaos")),
    )
    out_specs = P("chaos", "space")
    return jax.shard_map(local, mesh=mesh, in_specs=in_specs, out_specs=out_specs, check_vma=False)
```

```python
import functools

import jax
import jax.numpy as jnp
import numpy as np
from jax import lax
from jax.experimental import pallas as pl
from jax.experimental.pallas import tpu as pltpu
from jax.sharding import PartitionSpec as P

ELEM_NODES = 64
LANES = 128
FACE = 16
VMEM_LIMIT = 56 * 1024 * 1024
NT = (((1,), (1,)), ((), ()))
NN = (((1,), (0,)), ((), ()))
MESH = pl.DeviceIdType.MESH


def face_nodes():
    node_rows = []
    for side_idx in range(6):
        normal_axis = side_idx // 2
        plane_level = 3 * (side_idx % 2)
        row_nodes = []
        for first_coord in range(4):
            for second_coord in range(4):
                position = [first_coord, second_coord]
                position.insert(normal_axis, plane_level)
                row_nodes.append(16 * position[0] + 4 * position[1] + position[2])
        node_rows.append(row_nodes)
    return np.array(node_rows, dtype=np.int32)


def face_select():
    table = np.zeros((LANES, 2 * LANES), np.float32)
    for side, row in enumerate(face_nodes()):
        for point, node in enumerate(row):
            for half in range(2):
                table[half * ELEM_NODES + node, half * LANES + side * FACE + point] = 1.0
    return jnp.asarray(table, jnp.bfloat16)


def mm(a, b, dims=NN):
    return lax.dot_general(a, b, dims, preferred_element_type=jnp.float32)


def iota(shape, dim):
    return lax.broadcasted_iota(jnp.int32, shape, dim)


def hot(mask):
    return jnp.where(mask, 1.0, 0.0).astype(jnp.bfloat16)


def trade(x):
    group = iota((8, LANES), 1) // FACE
    for k in (1, 2, 4):
        upper = group // k % 2 == 1
        y = [None] * 8
        for v in range(8):
            if v & k:
                continue
            low, high = x[v], x[v + k]
            if high is not None:
                y[v] = jnp.where(upper, pltpu.roll(high, FACE * k, 1), low)
                y[v + k] = jnp.where(upper, high, pltpu.roll(low, LANES - FACE * k, 1))
            elif low is not None:
                y[v] = jnp.where(upper, 0.0, low)
                y[v + k] = jnp.where(upper, 0.0, pltpu.roll(low, LANES - FACE * k, 1))
        x = y
    return x


def to_items(turn, pad, count, store):
    for a in range(pad // 8):
        y = trade([turn[pl.ds(8 * a + b, 8, stride=pad), :] for b in range(8)])
        for g in range(0, count, 2):
            store(g, a, jnp.concatenate([y[g], y[g + 1]], axis=0).astype(jnp.bfloat16))


def to_tiles(load, count, turn, pad):
    for a in range(pad // 8):
        x = []
        for g in range(0, count, 2):
            both = load(g, a)
            x += [both[:8], both[8:]]
        y = trade(x + [None] * (8 - count))
        for b in range(8):
            turn[pl.ds(8 * a + b, 8, stride=pad), :] = y[b]


def face_row(elem, side):
    return lax.div(elem, 8) * 48 + side * 8 + lax.rem(elem, 2) * 4 + lax.div(lax.rem(elem, 8), 2)


def at_rows(start, count):
    return pl.ds(pl.multiple_of(start, 16), count)


def lanes_of(a):
    return slice(a * LANES, (a + 1) * LANES)


def column(row):
    size = row.shape[1]
    eye = iota((size, size), 0) == iota((size, size), 1)
    return jnp.sum(jnp.where(eye, row, 0), axis=1, keepdims=True)


def split_rows(part):
    high = part // 16 * 16
    return high, part - high, high + 16


def greet(axes):
    barrier = pltpu.get_barrier_semaphore()
    for axis, count in axes:
        me = lax.axis_index(axis)
        for d in range(1, count):
            pl.semaphore_signal(barrier, 1, device_id={axis: lax.rem(me + d, count)}, device_id_type=MESH)


def meet(axes):
    pl.semaphore_wait(pltpu.get_barrier_semaphore(), sum(count - 1 for _, count in axes))


def send(src, dst, sems, d, axis, peer):
    copy = pltpu.make_async_remote_copy(
        src_ref=src, dst_ref=dst, send_sem=sems.at[0, d - 1], recv_sem=sems.at[1, d - 1],
        device_id={axis: peer}, device_id_type=MESH)
    copy.start()
    return copy


def finish(copies):
    for copy in copies:
        copy.wait()


def pack(load, store, tail_ref, part, width):
    high, low, _ = split_rows(part)
    for q in range(16):
        upper, lower = load(q)
        store(slice(q * high, (q + 1) * high), upper)
        tail_ref[q * low:(q + 1) * low, :] = lower.astype(jnp.float32)
    store(slice(16 * high, 16 * part), tail_ref[...].astype(jnp.bfloat16))


def mix(coupling_ref, block, weights):
    total = weights[0:1] * block.astype(jnp.float32)
    for k in range(coupling_ref.shape[0]):
        total = total + weights[k + 1:k + 2] * mm(coupling_ref[k], block)
    return total.astype(jnp.bfloat16)


def slot_ids(requests, n, cap, faces):
    lane = iota((1, LANES), 1)
    return lax.rem(lane // cap, n) * faces + requests


def head_kernel(
    field_ref, stiff_ref, kl_ref, triple_ref, value_ref, index_ref, die_ref, int_ref, sel_ref,
    coupling_out, out_ref, proj_out, int_out, share_out, ask_out, die_diag, int_diag,
    msg, rows, sent, wide, block_ref, faces_ref, table_ref, slots, recv, picked, fp, stiff, die_faces, items, turn, tail_ref,
    share_sem, ask_sem, field_sem, slot_sem, pick_sem, *, n, ns, cap, faces,
):
    f32, bf16 = jnp.float32, jnp.bfloat16
    me_c, me_s = lax.axis_index("chaos"), lax.axis_index("space")
    axes = (("chaos", n), ("space", ns))
    greet(axes)
    part, local_nodes = field_ref.shape
    nodes = local_nodes // n
    width = nodes // 16
    per = width // LANES
    high, low, pad = split_rows(part)
    wide_lanes = pad * FACE
    modes, all_rows, _ = coupling_out.shape
    sel = sel_ref[...]

    index = index_ref[...]
    owner, seg_face = index[0:1], index[1:2]
    segs = owner.shape[1]
    r, c = iota((segs, segs), 0), iota((segs, segs), 1)
    owner_col, face_col = column(owner), column(seg_face)
    same = owner_col == owner
    rank_row = jnp.sum(jnp.where(same & (r < c), 1, 0), axis=0, keepdims=True)
    rank_col = jnp.sum(jnp.where(same & (c < r), 1, 0), axis=1, keepdims=True)
    base = me_c * (n * cap)
    lane_row = base + lax.rem(owner, n) * cap + rank_row
    lane_col = base + lax.rem(owner_col, n) * cap + rank_col
    left = hot(iota((16, segs), 0) == lax.div(owner, n))
    request = mm(left, jnp.where(c == lane_col, face_col, 0).astype(f32).astype(bf16))
    msg[...] = jnp.zeros(msg.shape, jnp.int32)
    msg[:ns, :] = request[:ns].astype(jnp.int32)
    msg[ns:ns + 1, :] = lax.div(owner, n) * LANES + lane_row
    msg[ns + 1:ns + 2, :] = index[2:3]
    meet(axes)
    share_out[me_c] = msg[...]
    copies = []
    for d in range(1, n):
        copies.append(send(msg, share_out.at[me_c], share_sem, d, "chaos", lax.rem(me_c + d, n)))

    field_copies = []
    for d in range(1, n + 1):
        peer = lax.rem(me_c + d, n)
        start = peer * nodes

        def load(q):
            cols = pl.ds(pl.multiple_of(start + q * width, LANES), width)
            return field_ref[:high, cols], field_ref[high:part, cols]

        def store(where, value):
            if d < n:
                sent[peer, where, :] = value
            else:
                wide[me_c, where, :] = value

        pack(load, store, tail_ref, part, width)
        if d < n:
            field_copies.append(send(sent.at[peer], wide.at[me_c], field_sem, d, "chaos", peer))
    finish(copies)

    total = share_out[0, :ns, :]
    for i in range(1, n):
        total = total + share_out[i, :ns, :]
    for s in range(ns):
        rows[s] = jnp.broadcast_to(total[s:s + 1, :], (8, LANES))
    ask_out[me_s] = rows[me_s]
    copies = []
    for d in range(1, ns):
        peer = lax.rem(me_s + d, ns)
        copies.append(send(rows.at[peer], ask_out.at[me_s], ask_sem, d, "space", peer))

    block_ref[...] = jnp.zeros(block_ref.shape, bf16)
    pairs = nodes // LANES
    blocks = pairs // 4

    def face_step(p, carry):
        for w in range(2):
            at = 2 * p + w
            for u in range(4):
                cols = pl.ds(pl.multiple_of((at * 4 + u) * LANES, LANES), LANES)
                block_ref[w, u * pad:u * pad + part, :] = field_ref[:, cols]
            found = mm(block_ref[w], sel)
            turn[w, :4 * pad] = found[:, :LANES]
            turn[w, 4 * pad:] = found[:, LANES:]

            def store(g, a, value):
                faces_ref[at_rows(at * 48 + g * 8, 16), lanes_of(a)] = value

            to_items(turn.at[w], pad, 6, store)
        return carry

    lax.fori_loop(0, n * blocks // 2, face_step, 0)
    elem_rows = blocks * 48
    for i in range(n):
        code = column(share_out[i, ns + 1:ns + 2, :])
        pick = hot(iota((LANES, elem_rows), 1) == code)
        found = mm(pick[:faces], faces_ref[i * elem_rows:(i + 1) * elem_rows, :])
        table_ref[i * faces:(i + 1) * faces, :] = found.astype(bf16)
    finish(copies)

    slot_copies = []
    for d in range(1, ns + 1):
        peer = lax.rem(me_s + d, ns)
        ids = column(slot_ids(ask_out[peer, 0:1, :], n, cap, faces))
        found = mm(hot(iota((LANES, n * faces), 1) == ids), table_ref[...]).astype(bf16)
        if d < ns:
            slots[peer] = found
            slot_copies.append(send(slots.at[peer], recv.at[me_s], slot_sem, d, "space", peer))
        else:
            recv[me_s] = found

    groups = die_diag.shape[0]
    lane_item = iota((FACE, LANES), 1) // FACE
    for mortar_ref, diag in ((die_ref, die_diag), (int_ref, int_diag)):
        for blk in range(groups // 8):
            for half in range(2):
                y = trade([
                    mortar_ref[blk * 64 + g // 2 * 16:blk * 64 + g // 2 * 16 + 16, lanes_of(half)].astype(f32)[
                        g % 2 * 8:g % 2 * 8 + 8] for g in range(8)
                ])
                for m in range(8):
                    turn[blk % 2, pl.ds(half * 8 + m, 8, stride=FACE), :] = y[m]
            for t in range(8):
                mat = turn[blk % 2, t * FACE:(t + 1) * FACE, :]
                for g in range(8):
                    diag[blk * 8 + t, g * FACE:(g + 1) * FACE, :] = jnp.where(lane_item == g, mat, 0.0).astype(bf16)

    triples = triple_ref[...]
    value = value_ref[...]
    key, col = triples[0:1], triples[1:2]
    coarse = value.astype(bf16).astype(f32)
    at_col = iota((all_rows, key.shape[1]), 0) == col
    right = jnp.concatenate(
        [jnp.where(at_col, coarse, 0.0).astype(bf16), jnp.where(at_col, value - coarse, 0.0).astype(bf16)], axis=0
    )

    def mode_step(k, carry):
        at_row = hot(iota((all_rows, key.shape[1]), 0) + k * all_rows == key)
        both = mm(at_row, right, NT)
        coupling_out[k] = (both[:, :all_rows] + both[:, all_rows:]).astype(bf16)
        return carry

    lax.fori_loop(0, modes, mode_step, 0)

    elems = stiff_ref.shape[0]
    for t in range(ELEM_NODES // 2):
        block = stiff_ref[:, t * LANES:(t + 1) * LANES].astype(f32)
        stiff[pl.ds(2 * t, elems, stride=ELEM_NODES), :] = block
        stiff[pl.ds(2 * t + 1, elems, stride=ELEM_NODES), :] = pltpu.roll(block, ELEM_NODES, 1)

    finish(slot_copies)
    pick_copies = []
    everything = recv[...].reshape(ns * LANES, wide_lanes)
    for d in range(1, n + 1):
        peer = lax.rem(me_c + d, n)
        spot = column(share_out[peer, ns:ns + 1, :])
        found = mm(hot(iota((segs, ns * LANES), 1) == spot), everything).astype(bf16)
        if d < n:
            picked[peer] = found
            pick_copies.append(send(picked.at[peer], int_out.at[me_c], pick_sem, d, "chaos", peer))
        else:
            int_out[me_c] = found

    finish(field_copies)
    keep = iota((16, width), 0) < low
    for i in range(n):
        tail_ref[...] = wide[i, 16 * high:, :].astype(f32)
        for q in range(16):
            first = min(q * low, 16 * low - 16)
            tail = tail_ref[first:first + 16, :]
            if first < q * low:
                tail = pltpu.roll(tail, 16 - (q * low - first), 0)
            tail = jnp.where(keep, tail, 0.0).astype(bf16)
            for h in range(per):
                cols = slice(h * LANES, (h + 1) * LANES)
                fp[q * per + h, i * pad:i * pad + high, :] = wide[i, q * high:(q + 1) * high, cols]
                fp[q * per + h, i * pad + high:(i + 1) * pad, :] = tail[:, cols]

    lower = iota((ELEM_NODES, LANES), 1) < ELEM_NODES

    def element_step(p, carry):
        block = jnp.concatenate([fp[4 * p + u] for u in range(4)], axis=1)
        spread = jnp.where(iota((elems, 512), 1) // ELEM_NODES + 8 * p == iota((elems, 512), 0), 1.0, 0.0)
        weights = lax.dot_general(
            kl_ref[...], spread, NN, precision=lax.Precision.HIGHEST, preferred_element_type=f32)
        mixed = mix(coupling_out, block, weights)
        for h in range(4):
            at = pl.multiple_of((4 * p + h) * LANES, LANES)
            even = jnp.where(lower, stiff[pl.ds(at, ELEM_NODES), :], 0.0)
            odd = pltpu.roll(stiff[pl.ds(at + ELEM_NODES, ELEM_NODES), :], ELEM_NODES, 1)
            odd = jnp.where(lower, 0.0, odd)
            diag = jnp.concatenate([even, odd], axis=0).astype(bf16)
            out_ref[4 * p + h] = mm(mixed[:, lanes_of(h)], diag, NT)
        return carry

    lax.fori_loop(0, pairs // 4, element_step, 0)

    def die_step(blk, carry):
        for u in range(4):
            found = mm(fp[4 * blk + u], sel)
            for i in range(n):
                for h in range(2):
                    turn[i, (4 * h + u) * pad:(4 * h + u + 1) * pad] = found[i * pad:(i + 1) * pad, lanes_of(h)]
        for i in range(n):
            def store(g, a, value):
                die_faces[i, at_rows(blk * 48 + g * 8, 16), lanes_of(a)] = value

            to_items(turn.at[i], pad, 6, store)
        return carry

    lax.fori_loop(0, blocks, die_step, 0)
    pick = hot(iota((segs, elem_rows), 1) == column(index[3:4]))
    for i in range(n):
        items[:segs] = mm(pick, die_faces[i])

        def project_step(blk, carry):
            to_tiles(lambda g, a: items[at_rows(blk * 64 + g * 8, 16), lanes_of(a)], 8, turn.at[0], pad)
            for t in range(8):
                proj_out[blk * 8 + t, i * pad:(i + 1) * pad, :] = turn[0, t * pad:(t + 1) * pad].astype(bf16)
            return carry

        lax.fori_loop(0, groups // 8, project_step, 0)

    def mortar_step(g, carry):
        proj_out[g] = mm(proj_out[g], die_diag[g], NT).astype(bf16)
        return carry

    lax.fori_loop(0, groups, mortar_step, 0, unroll=4)
    finish(pick_copies)


def tail_kernel(
    faces_ref, proj_ref, die_diag, int_diag, coupling_ref, coef_ref, local_ref, index_ref, share_ref, ask_ref, sel_ref,
    returned, delta_out,
    back_send, back_recv, die_back, out_send, slots, recv, items, turn, int_turn, die_turn, stage, tail_ref,
    back_sem, out_sem, slot_sem, *, n, ns, cap, faces, part,
):
    f32, bf16 = jnp.float32, jnp.bfloat16
    me_c, me_s = lax.axis_index("chaos"), lax.axis_index("space")
    axes = (("chaos", n), ("space", ns))
    greet(axes)
    groups, all_rows, _ = proj_ref.shape
    pairs = local_ref.shape[0]
    high, low, pad = split_rows(part)
    wide_lanes = pad * FACE
    width = returned.shape[2]
    per = width // LANES
    segs = index_ref.shape[1]
    sel = sel_ref[...]

    def flux_step(blk, carry):
        for i in range(n):
            to_tiles(
                lambda g, a: faces_ref[i, at_rows(blk * 64 + g * 8, 16), lanes_of(a)].astype(f32), 8, turn.at[i], pad)

        for r in range(2):
            jumps = []
            for h in range(4):
                t = 4 * r + h
                face = jnp.concatenate([turn[i, t * pad:(t + 1) * pad] for i in range(n)], axis=0).astype(bf16)
                own = mm(face, int_diag[blk * 8 + t], NT)
                jumps.append((proj_ref[blk * 8 + t].astype(f32) - own).astype(bf16))
            lane = iota((segs, 512), 1)
            seg = blk * 64 + lane % LANES // FACE * 8 + 4 * r + lane // LANES
            weights = mm(coef_ref[...], hot(seg == iota((segs, 512), 0)))
            flux = mix(coupling_ref, jnp.concatenate(jumps, axis=1), weights)
            for h in range(4):
                t = 4 * r + h
                own = flux[:, lanes_of(h)]
                int_side = mm(own, int_diag[blk * 8 + t])
                die_side = mm(own, die_diag[blk * 8 + t])
                for i in range(n):
                    int_turn[i, t * pad:(t + 1) * pad] = int_side[i * pad:(i + 1) * pad]
                    die_turn[i, t * pad:(t + 1) * pad] = die_side[i * pad:(i + 1) * pad]
        for i in range(n):
            def store_int(g, a, value):
                back_send[i, at_rows(blk * 64 + g * 8, 16), lanes_of(a)] = value

            def store_die(g, a, value):
                die_back[i, at_rows(blk * 64 + g * 8, 16), lanes_of(a)] = value

            to_items(int_turn.at[i], pad, 8, store_int)
            to_items(die_turn.at[i], pad, 8, store_die)
        return carry

    lax.fori_loop(0, groups // 8, flux_step, 0)
    meet(axes)
    back_copies = []
    for d in range(1, n):
        peer = lax.rem(me_c + d, n)
        back_copies.append(send(back_send.at[peer], back_recv.at[me_c], back_sem, d, "chaos", peer))
    back_recv[me_c] = back_send[me_c]

    blocks = pairs // 4
    elem_rows = blocks * 48
    place = hot(iota((elem_rows, segs), 0) == index_ref[3:4, :])

    def nodal(blk, own):
        to_tiles(lambda g, a: items[at_rows(blk * 48 + g * 8, 16), lanes_of(a)], 6, own, pad)
        both = jnp.concatenate([own[:4 * pad], own[4 * pad:]], axis=1).astype(bf16)
        return mm(both, sel, NT)

    out_copies = []
    for d in range(1, n + 1):
        peer = lax.rem(me_c + d, n)
        items[...] = mm(place, die_back[peer])
        out_block = out_send.at[peer] if d < n else returned.at[me_c]

        def out_step(b, carry):
            for w in range(2):
                blk = 2 * b + w
                added = nodal(blk, turn.at[w])
                for u in range(4):
                    own = local_ref[blk * 4 + u, at_rows(peer * pad, pad), :] + added[u * pad:(u + 1) * pad]
                    q = (blk * 4 + u) // per
                    out_block[at_rows(q * high, high), lanes_of(u % per)] = own[:high].astype(bf16)
                    stage[q, :, lanes_of(u % per)] = own[high:]
            return carry

        lax.fori_loop(0, blocks // 2, out_step, 0)
        for q in range(16):
            tail_ref[q * low:(q + 1) * low, :] = stage[q, :low, :]
        out_block[16 * high:, :] = tail_ref[...].astype(bf16)
        if d < n:
            out_copies.append(send(out_send.at[peer], returned.at[me_c], out_sem, d, "chaos", peer))

    finish(back_copies)
    everything = back_recv[...].reshape(n * segs, wide_lanes)
    spots = jnp.concatenate([share_ref[i, ns:ns + 1, :] for i in range(n)], axis=1)
    slot_copies = []
    for d in range(1, ns + 1):
        peer = lax.rem(me_s + d, ns)
        found = mm(hot(iota((LANES, n * segs), 0) + peer * LANES == spots), everything).astype(bf16)
        if d < ns:
            slots[peer] = found
            slot_copies.append(send(slots.at[peer], recv.at[me_s], slot_sem, d, "space", peer))
        else:
            recv[me_s] = found
    finish(slot_copies)

    ids = jnp.concatenate([slot_ids(ask_ref[s, 0:1, :], n, cap, faces) for s in range(ns)], axis=1)
    everything = recv[...].reshape(ns * LANES, wide_lanes)
    summed = mm(hot(iota((n * faces, ns * LANES), 0) == ids), everything).astype(bf16)
    for i in range(n):
        code = share_ref[i, ns + 1:ns + 2, :][:, :faces]
        items[...] = mm(hot(iota((elem_rows, faces), 0) == code), summed[i * faces:(i + 1) * faces])

        def delta_step(b, carry):
            for w in range(2):
                blk = 2 * b + w
                added = nodal(blk, turn.at[w])
                for u in range(4):
                    delta_out[i * pairs + blk * 4 + u] = added[u * pad:(u + 1) * pad]
            return carry

        lax.fori_loop(0, blocks // 2, delta_step, 0)
    finish(out_copies)


def receive_kernel(in_ref, delta_ref, out_ref, tail_ref):
    part, nodes = out_ref.shape
    high, low, _ = split_rows(part)
    width = nodes // 16
    per = width // LANES
    tail_ref[...] = in_ref[0, 16 * high:, :].astype(jnp.float32)
    for q in range(16):
        for h in range(per):
            cols = slice(q * width + h * LANES, q * width + (h + 1) * LANES)
            own = slice(h * LANES, (h + 1) * LANES)
            delta = delta_ref[q * per + h]
            upper = in_ref[0, q * high:(q + 1) * high, own].astype(jnp.float32)
            out_ref[:high, cols] = (upper - delta[:high]).astype(jnp.bfloat16)
            lower = tail_ref[q * low:(q + 1) * low, own]
            out_ref[high:part, cols] = (lower - delta[high:part]).astype(jnp.bfloat16)


def call(kernel, outs, args, scratch, collective_id):
    moved = sum(x.size * x.dtype.itemsize for x in (*args, *outs))
    return pl.pallas_call(
        kernel,
        out_shape=outs,
        in_specs=[pl.BlockSpec(memory_space=pltpu.VMEM)] * len(args),
        out_specs=tuple(pl.BlockSpec(memory_space=pltpu.VMEM) for _ in outs),
        scratch_shapes=scratch,
        compiler_params=pltpu.CompilerParams(
            collective_id=collective_id, has_side_effects=True, vmem_limit_bytes=VMEM_LIMIT
        ),
        cost_estimate=pl.CostEstimate(flops=0, bytes_accessed=moved, transcendentals=0),
    )(*args)


def local(
    field,
    stiffness,
    kl_coef,
    triple_mode,
    triple_row,
    triple_col,
    triple_value,
    die_elem,
    die_side,
    seg_owner,
    seg_face,
    die_mortar,
    int_mortar,
    bump_coef,
    int_elem,
    int_side,
):
    n, ns = lax.axis_size("chaos"), lax.axis_size("space")
    part, local_nodes = field.shape
    nodes = local_nodes // n
    segs = die_elem.shape[0]
    cap = max(2, 2 * segs // (n * ns))
    faces = int_elem.shape[0]
    pairs = nodes // LANES
    modes = bump_coef.shape[1] - 1
    high, low, pad = split_rows(part)
    rows = n * pad
    lanes = pad * FACE
    groups = segs // 8
    width = nodes // 16
    bf16, f32, i32 = jnp.bfloat16, jnp.float32, jnp.int32
    sel = face_select()

    index = jnp.stack([
        seg_owner, seg_face, jnp.pad(face_row(int_elem, int_side), (0, segs - faces)), face_row(die_elem, die_side),
    ])
    triples = jnp.stack([
        triple_mode * rows + triple_row // part * pad + triple_row % part, triple_col // part * pad + triple_col % part,
    ])
    height = (ns + 2 + 7) // 8 * 8
    packed = (n, 16 * part, width)

    def sems(count):
        return pltpu.SemaphoreType.DMA((2, count - 1))

    coupling, local_out, proj, int_faces, shared, asked, die_diag, int_diag = call(
        functools.partial(head_kernel, n=n, ns=ns, cap=cap, faces=faces),
        (
            jax.ShapeDtypeStruct((modes, rows, rows), bf16),
            jax.ShapeDtypeStruct((pairs, rows, LANES), f32),
            jax.ShapeDtypeStruct((groups, rows, LANES), bf16),
            jax.ShapeDtypeStruct((n, segs, lanes), bf16),
            jax.ShapeDtypeStruct((n, height, LANES), i32),
            jax.ShapeDtypeStruct((ns, 8, LANES), i32),
            jax.ShapeDtypeStruct((groups, LANES, LANES), bf16),
            jax.ShapeDtypeStruct((groups, LANES, LANES), bf16),
        ),
        (
            field, stiffness, kl_coef, triples, triple_value.reshape(1, -1), index,
            die_mortar, int_mortar, sel,
        ),
        (
            pltpu.VMEM((height, LANES), i32),
            pltpu.VMEM((ns, 8, LANES), i32),
            pltpu.VMEM(packed, bf16),
            pltpu.VMEM(packed, bf16),
            pltpu.VMEM((2, 4 * pad, LANES), bf16),
            pltpu.VMEM((n * pairs * 12, lanes), bf16),
            pltpu.VMEM((n * faces, lanes), bf16),
            pltpu.VMEM((ns, LANES, lanes), bf16),
            pltpu.VMEM((ns, LANES, lanes), bf16),
            pltpu.VMEM((n, segs, lanes), bf16),
            pltpu.VMEM((pairs, rows, LANES), bf16),
            pltpu.VMEM((2 * pairs * ELEM_NODES, LANES), f32),
            pltpu.VMEM((n, pairs * 12, lanes), bf16),
            pltpu.VMEM((segs, lanes), f32),
            pltpu.VMEM((n, 8 * pad, LANES), f32),
            pltpu.VMEM((16 * low, width), f32),
            sems(n), sems(ns), sems(n), sems(ns), sems(n),
        ),
        0,
    )
    returned, delta = call(
        functools.partial(tail_kernel, n=n, ns=ns, cap=cap, faces=faces, part=part),
        (
            jax.ShapeDtypeStruct(packed, bf16),
            jax.ShapeDtypeStruct((n * pairs, pad, LANES), f32),
        ),
        (int_faces, proj, die_diag, int_diag, coupling, bump_coef.T, local_out, index, shared, asked, sel),
        (
            pltpu.VMEM((n, segs, lanes), bf16),
            pltpu.VMEM((n, segs, lanes), bf16),
            pltpu.VMEM((n, segs, lanes), bf16),
            pltpu.VMEM(packed, bf16),
            pltpu.VMEM((ns, LANES, lanes), bf16),
            pltpu.VMEM((ns, LANES, lanes), bf16),
            pltpu.VMEM((pairs * 12, lanes), f32),
            pltpu.VMEM((n, 8 * pad, LANES), f32),
            pltpu.VMEM((n, 8 * pad, LANES), f32),
            pltpu.VMEM((n, 8 * pad, LANES), f32),
            pltpu.VMEM((16, 16, width), f32),
            pltpu.VMEM((16 * low, width), f32),
            sems(n), sems(n), sems(ns),
        ),
        1,
    )
    return pl.pallas_call(
        receive_kernel,
        out_shape=jax.ShapeDtypeStruct((part, local_nodes), bf16),
        grid=(n,),
        in_specs=[
            pl.BlockSpec((1, 16 * part, width), lambda c: (c, 0, 0)),
            pl.BlockSpec((pairs, pad, LANES), lambda c: (c, 0, 0)),
        ],
        out_specs=pl.BlockSpec((part, nodes), lambda c: (0, c)),
        scratch_shapes=[pltpu.VMEM((16 * low, width), f32)],
    )(returned, delta)


def solution(mesh):
    in_specs = (
        P("chaos", "space"),
        P(("space", "chaos"), None),
        P(None, ("space", "chaos")),
        P(),
        P(),
        P(),
        P(),
        P(("space", "chaos")),
        P(("space", "chaos")),
        P(("space", "chaos")),
        P(("space", "chaos")),
        P(("space", "chaos"), None),
        P(("space", "chaos"), None),
        P(("space", "chaos"), None),
        P(("space", "chaos")),
        P(("space", "chaos")),
    )
    out_specs = P("chaos", "space")
    return jax.shard_map(local, mesh=mesh, in_specs=in_specs, out_specs=out_specs, check_vma=False)
```

```python
import functools

import jax
import jax.numpy as jnp
import numpy as np
from jax import lax
from jax.experimental import pallas as pl
from jax.experimental.pallas import tpu as pltpu
from jax.sharding import PartitionSpec as P

ELEM_NODES = 64
LANES = 128
FACE = 16
VMEM_LIMIT = 56 * 1024 * 1024
NT = (((1,), (1,)), ((), ()))
NN = (((1,), (0,)), ((), ()))
TN = (((0,), (0,)), ((), ()))
MESH = pl.DeviceIdType.MESH


def face_nodes():
    node_rows = []
    for side_idx in range(6):
        normal_axis = side_idx // 2
        plane_level = 3 * (side_idx % 2)
        row_nodes = []
        for first_coord in range(4):
            for second_coord in range(4):
                position = [first_coord, second_coord]
                position.insert(normal_axis, plane_level)
                row_nodes.append(16 * position[0] + 4 * position[1] + position[2])
        node_rows.append(row_nodes)
    return np.array(node_rows, dtype=np.int32)


def face_select():
    table = np.zeros((LANES, 2 * LANES), np.float32)
    for side, row in enumerate(face_nodes()):
        for point, node in enumerate(row):
            for half in range(2):
                table[half * ELEM_NODES + node, half * LANES + side * FACE + point] = 1.0
    return jnp.asarray(table, jnp.bfloat16)


def mm(a, b, dims=NN):
    return lax.dot_general(a, b, dims, preferred_element_type=jnp.float32)


def iota(shape, dim):
    return lax.broadcasted_iota(jnp.int32, shape, dim)


def hot(mask):
    return jnp.where(mask, 1.0, 0.0).astype(jnp.bfloat16)


def trade(x):
    group = iota((8, LANES), 1) // FACE
    for k in (1, 2, 4):
        upper = group // k % 2 == 1
        y = [None] * 8
        for v in range(8):
            if v & k:
                continue
            low, high = x[v], x[v + k]
            if high is not None:
                y[v] = jnp.where(upper, pltpu.roll(high, FACE * k, 1), low)
                y[v + k] = jnp.where(upper, high, pltpu.roll(low, LANES - FACE * k, 1))
            elif low is not None:
                y[v] = jnp.where(upper, 0.0, low)
                y[v + k] = jnp.where(upper, 0.0, pltpu.roll(low, LANES - FACE * k, 1))
        x = y
    return x


def to_items(turn, pad, count, store):
    for a in range(pad // 8):
        y = trade([turn[pl.ds(8 * a + b, 8, stride=pad), :] for b in range(8)])
        for g in range(0, count, 2):
            store(g, a, jnp.concatenate([y[g], y[g + 1]], axis=0).astype(jnp.bfloat16))


def to_tiles(load, count, turn, pad):
    for a in range(pad // 8):
        x = []
        for g in range(0, count, 2):
            both = load(g, a)
            x += [both[:8], both[8:]]
        y = trade(x + [None] * (8 - count))
        for b in range(8):
            turn[pl.ds(8 * a + b, 8, stride=pad), :] = y[b]


def face_row(elem, side):
    return lax.div(elem, 8) * 48 + side * 8 + lax.rem(elem, 2) * 4 + lax.div(lax.rem(elem, 8), 2)


def at_rows(start, count):
    return pl.ds(pl.multiple_of(start, 16), count)


def lanes_of(a):
    return slice(a * LANES, (a + 1) * LANES)


def column(row):
    size = row.shape[1]
    eye = iota((size, size), 0) == iota((size, size), 1)
    return jnp.sum(jnp.where(eye, row, 0), axis=1, keepdims=True)


def split_rows(part):
    high = part // 16 * 16
    return high, part - high, high + 16


def greet(axes):
    barrier = pltpu.get_barrier_semaphore()
    for axis, count in axes:
        me = lax.axis_index(axis)
        for d in range(1, count):
            pl.semaphore_signal(barrier, 1, device_id={axis: lax.rem(me + d, count)}, device_id_type=MESH)


def meet(axes):
    pl.semaphore_wait(pltpu.get_barrier_semaphore(), sum(count - 1 for _, count in axes))


def send(src, dst, sems, d, axis, peer):
    copy = pltpu.make_async_remote_copy(
        src_ref=src, dst_ref=dst, send_sem=sems.at[0, d - 1], recv_sem=sems.at[1, d - 1],
        device_id={axis: peer}, device_id_type=MESH)
    copy.start()
    return copy


def finish(copies):
    for copy in copies:
        copy.wait()


def pack(load, store, tail_ref, part, width):
    high, low, _ = split_rows(part)
    for q in range(16):
        upper, lower = load(q)
        store(slice(q * high, (q + 1) * high), upper)
        tail_ref[q * low:(q + 1) * low, :] = lower.astype(jnp.float32)
    store(slice(16 * high, 16 * part), tail_ref[...].astype(jnp.bfloat16))


def mix(coupling_ref, block, weights):
    total = weights[0:1] * block.astype(jnp.float32)
    for k in range(coupling_ref.shape[0]):
        total = total + weights[k + 1:k + 2] * mm(coupling_ref[k], block)
    return total.astype(jnp.bfloat16)


def slot_ids(requests, n, cap, faces):
    lane = iota((1, LANES), 1)
    return lax.rem(lane // cap, n) * faces + requests


def row_of(ref):
    return ref[...].reshape(1, -1)


def whole_kernel(
    field_ref, stiff_ref, kl_ref, mode_ref, row_ref, col_ref, value_ref, die_elem_ref, die_side_ref, owner_ref,
    seg_face_ref, die_ref, int_ref, coef_ref, int_elem_ref, int_side_ref, sel_ref, back_sel_ref,
    out_ref,
    coupling_out, local_ref, proj_out, int_out, share_out, ask_out, die_diag, int_diag,
    msg, rows, sent, wide, block_ref, faces_ref, table_ref, slots, recv, picked, fp, stiff, die_faces, items, turn, tail_ref,
    back_send, back_recv, die_back, out_send, returned, back_slots, back_got, int_turn, die_turn, stage, delta_ref,
    share_sem, ask_sem, field_sem, slot_sem, pick_sem, back_sem, out_sem, back_slot_sem, *, n, ns, cap, faces,
):
    f32, bf16 = jnp.float32, jnp.bfloat16
    me_c, me_s = lax.axis_index("chaos"), lax.axis_index("space")
    axes = (("chaos", n), ("space", ns))
    greet(axes)
    part, local_nodes = field_ref.shape
    nodes = local_nodes // n
    width = nodes // 16
    per = width // LANES
    high, low, pad = split_rows(part)
    wide_lanes = pad * FACE
    modes, all_rows, _ = coupling_out.shape
    sel = sel_ref[...]

    owner, seg_face = row_of(owner_ref), row_of(seg_face_ref)
    die_row = face_row(row_of(die_elem_ref), row_of(die_side_ref))
    segs = owner.shape[1]
    r, c = iota((segs, segs), 0), iota((segs, segs), 1)
    owner_col, face_col = column(owner), column(seg_face)
    same = owner_col == owner
    rank_row = jnp.sum(jnp.where(same & (r < c), 1, 0), axis=0, keepdims=True)
    rank_col = jnp.sum(jnp.where(same & (c < r), 1, 0), axis=1, keepdims=True)
    base = me_c * (n * cap)
    lane_row = base + lax.rem(owner, n) * cap + rank_row
    lane_col = base + lax.rem(owner_col, n) * cap + rank_col
    left = hot(iota((16, segs), 0) == lax.div(owner, n))
    request = mm(left, jnp.where(c == lane_col, face_col, 0).astype(f32).astype(bf16))
    msg[...] = jnp.zeros(msg.shape, jnp.int32)
    msg[:ns, :] = request[:ns].astype(jnp.int32)
    msg[ns:ns + 1, :] = lax.div(owner, n) * LANES + lane_row
    msg[ns + 1:ns + 2, :faces] = face_row(row_of(int_elem_ref), row_of(int_side_ref))
    field_copies = []
    for d in range(1, n + 1):
        peer = lax.rem(me_c + d, n)
        start = peer * nodes

        def load(q):
            cols = pl.ds(pl.multiple_of(start + q * width, LANES), width)
            return field_ref[:high, cols], field_ref[high:part, cols]

        def store(where, value):
            if d < n:
                sent[peer, where, :] = value
            else:
                wide[me_c, where, :] = value

        pack(load, store, tail_ref, part, width)
        if d == 1:
            meet(axes)
            share_out[me_c] = msg[...]
            copies = [
                send(msg, share_out.at[me_c], share_sem, e, "chaos", lax.rem(me_c + e, n)) for e in range(1, n)
            ]
        if d < n:
            field_copies.append(send(sent.at[peer], wide.at[me_c], field_sem, d, "chaos", peer))
    finish(copies)

    total = share_out[0, :ns, :]
    for i in range(1, n):
        total = total + share_out[i, :ns, :]
    for s in range(ns):
        rows[s] = jnp.broadcast_to(total[s:s + 1, :], (8, LANES))
    ask_out[me_s] = rows[me_s]
    copies = []
    for d in range(1, ns):
        peer = lax.rem(me_s + d, ns)
        copies.append(send(rows.at[peer], ask_out.at[me_s], ask_sem, d, "space", peer))

    block_ref[...] = jnp.zeros(block_ref.shape, bf16)
    pairs = nodes // LANES
    blocks = pairs // 4

    def face_step(p, carry):
        for w in range(4):
            at = 4 * p + w
            for u in range(4):
                cols = pl.ds(pl.multiple_of((at * 4 + u) * LANES, LANES), LANES)
                block_ref[w, u * pad:u * pad + part, :] = field_ref[:, cols]
            found = mm(block_ref[w], sel)
            turn[w, :4 * pad] = found[:, :LANES]
            turn[w, 4 * pad:] = found[:, LANES:]

            def store(g, a, value):
                faces_ref[at_rows(at * 48 + g * 8, 16), lanes_of(a)] = value

            to_items(turn.at[w], pad, 6, store)
        return carry

    lax.fori_loop(0, n * blocks // 4, face_step, 0)
    elem_rows = blocks * 48
    for i in range(n):
        code = column(share_out[i, ns + 1:ns + 2, :])
        pick = hot(iota((LANES, elem_rows), 1) == code)
        found = mm(pick[:faces], faces_ref[i * elem_rows:(i + 1) * elem_rows, :])
        table_ref[i * faces:(i + 1) * faces, :] = found.astype(bf16)
    finish(copies)

    slot_copies = []
    for d in range(1, ns + 1):
        peer = lax.rem(me_s + d, ns)
        ids = column(slot_ids(ask_out[peer, 0:1, :], n, cap, faces))
        found = mm(hot(iota((LANES, n * faces), 1) == ids), table_ref[...]).astype(bf16)
        if d < ns:
            slots[peer] = found
            slot_copies.append(send(slots.at[peer], recv.at[me_s], slot_sem, d, "space", peer))
        else:
            recv[me_s] = found

    groups = die_diag.shape[0]
    lane_item = iota((FACE, LANES), 1) // FACE
    for mortar_ref, diag in ((die_ref, die_diag), (int_ref, int_diag)):
        for blk in range(groups // 8):
            for half in range(2):
                y = trade([
                    mortar_ref[blk * 64 + g // 2 * 16:blk * 64 + g // 2 * 16 + 16, lanes_of(half)].astype(f32)[
                        g % 2 * 8:g % 2 * 8 + 8] for g in range(8)
                ])
                for m in range(8):
                    turn[blk % 2, pl.ds(half * 8 + m, 8, stride=FACE), :] = y[m]
            for t in range(8):
                mat = turn[blk % 2, t * FACE:(t + 1) * FACE, :]
                for g in range(8):
                    diag[blk * 8 + t, g * FACE:(g + 1) * FACE, :] = jnp.where(lane_item == g, mat, 0.0).astype(bf16)

    def padded(chaos):
        return chaos + sum(jnp.where(chaos >= i * part, pad - part, 0) for i in range(1, n))

    value = row_of(value_ref)
    key = row_of(mode_ref) * all_rows + padded(row_of(row_ref))
    col = padded(row_of(col_ref))
    coarse = value.astype(bf16).astype(f32)
    at_col = iota((all_rows, key.shape[1]), 0) == col
    right = jnp.concatenate(
        [jnp.where(at_col, coarse, 0.0).astype(bf16), jnp.where(at_col, value - coarse, 0.0).astype(bf16)], axis=0
    )

    def mode_step(k, carry):
        at_row = hot(iota((all_rows, key.shape[1]), 0) + k * all_rows == key)
        both = mm(at_row, right, NT)
        coupling_out[k] = (both[:, :all_rows] + both[:, all_rows:]).astype(bf16)
        return carry

    lax.fori_loop(0, modes, mode_step, 0)

    elems = stiff_ref.shape[0]
    for t in range(ELEM_NODES // 2):
        block = stiff_ref[:, t * LANES:(t + 1) * LANES].astype(f32)
        stiff[pl.ds(2 * t, elems, stride=ELEM_NODES), :] = block
        stiff[pl.ds(2 * t + 1, elems, stride=ELEM_NODES), :] = pltpu.roll(block, ELEM_NODES, 1)

    finish(slot_copies)
    pick_copies = []
    everything = recv[...].reshape(ns * LANES, wide_lanes)
    for d in range(1, n + 1):
        peer = lax.rem(me_c + d, n)
        spot = column(share_out[peer, ns:ns + 1, :])
        found = mm(hot(iota((segs, ns * LANES), 1) == spot), everything).astype(bf16)
        if d < n:
            picked[peer] = found
            pick_copies.append(send(picked.at[peer], int_out.at[me_c], pick_sem, d, "chaos", peer))
        else:
            int_out[me_c] = found

    finish(field_copies)
    keep = iota((16, width), 0) < low
    for i in range(n):
        tail_ref[...] = wide[i, 16 * high:, :].astype(f32)
        for q in range(16):
            first = min(q * low, 16 * low - 16)
            tail = tail_ref[first:first + 16, :]
            if first < q * low:
                tail = pltpu.roll(tail, 16 - (q * low - first), 0)
            tail = jnp.where(keep, tail, 0.0).astype(bf16)
            for h in range(per):
                cols = slice(h * LANES, (h + 1) * LANES)
                fp[q * per + h, i * pad:i * pad + high, :] = wide[i, q * high:(q + 1) * high, cols]
                fp[q * per + h, i * pad + high:(i + 1) * pad, :] = tail[:, cols]

    lower = iota((ELEM_NODES, LANES), 1) < ELEM_NODES

    def element_step(p, carry):
        block = jnp.concatenate([fp[4 * p + u] for u in range(4)], axis=1)
        spread = jnp.where(iota((elems, 512), 1) // ELEM_NODES + 8 * p == iota((elems, 512), 0), 1.0, 0.0)
        weights = lax.dot_general(
            kl_ref[...], spread, NN, precision=lax.Precision.HIGHEST, preferred_element_type=f32)
        mixed = mix(coupling_out, block, weights)
        for h in range(4):
            at = pl.multiple_of((4 * p + h) * LANES, LANES)
            even = jnp.where(lower, stiff[pl.ds(at, ELEM_NODES), :], 0.0)
            odd = pltpu.roll(stiff[pl.ds(at + ELEM_NODES, ELEM_NODES), :], ELEM_NODES, 1)
            odd = jnp.where(lower, 0.0, odd)
            diag = jnp.concatenate([even, odd], axis=0).astype(bf16)
            local_ref[4 * p + h] = mm(mixed[:, lanes_of(h)], diag, NT)
        return carry

    lax.fori_loop(0, pairs // 4, element_step, 0)

    def die_step(blk, carry):
        for u in range(4):
            found = mm(fp[4 * blk + u], sel)
            for i in range(n):
                for h in range(2):
                    turn[i, (4 * h + u) * pad:(4 * h + u + 1) * pad] = found[i * pad:(i + 1) * pad, lanes_of(h)]
        for i in range(n):
            def store(g, a, value):
                die_faces[i, at_rows(blk * 48 + g * 8, 16), lanes_of(a)] = value

            to_items(turn.at[i], pad, 6, store)
        return carry

    lax.fori_loop(0, blocks, die_step, 0)
    pick = hot(iota((segs, elem_rows), 1) == column(die_row))
    for i in range(n):
        items[:segs] = mm(pick, die_faces[i])

        def project_step(blk, carry):
            to_tiles(lambda g, a: items[at_rows(blk * 64 + g * 8, 16), lanes_of(a)], 8, turn.at[0], pad)
            for t in range(8):
                proj_out[blk * 8 + t, i * pad:(i + 1) * pad, :] = turn[0, t * pad:(t + 1) * pad].astype(bf16)
            return carry

        lax.fori_loop(0, groups // 8, project_step, 0)

    def mortar_step(g, carry):
        proj_out[g] = mm(proj_out[g], die_diag[g], NT).astype(bf16)
        return carry

    lax.fori_loop(0, groups, mortar_step, 0, unroll=4)
    finish(pick_copies)
    back_sel = back_sel_ref[...]

    def flux_step(blk, carry):
        for i in range(n):
            to_tiles(
                lambda g, a: int_out[i, at_rows(blk * 64 + g * 8, 16), lanes_of(a)].astype(f32), 8, turn.at[i], pad)

        for r in range(2):
            jumps = []
            for h in range(4):
                t = 4 * r + h
                face = jnp.concatenate([turn[i, t * pad:(t + 1) * pad] for i in range(n)], axis=0).astype(bf16)
                own = mm(face, int_diag[blk * 8 + t], NT)
                jumps.append((proj_out[blk * 8 + t].astype(f32) - own).astype(bf16))
            lane = iota((segs, 512), 1)
            seg = blk * 64 + lane % LANES // FACE * 8 + 4 * r + lane // LANES
            weights = lax.dot_general(
                coef_ref[...], hot(seg == iota((segs, 512), 0)), TN, preferred_element_type=f32)
            flux = mix(coupling_out, jnp.concatenate(jumps, axis=1), weights)
            for h in range(4):
                t = 4 * r + h
                own = flux[:, lanes_of(h)]
                int_side = mm(own, int_diag[blk * 8 + t])
                die_side = mm(own, die_diag[blk * 8 + t])
                for i in range(n):
                    int_turn[i, t * pad:(t + 1) * pad] = int_side[i * pad:(i + 1) * pad]
                    die_turn[i, t * pad:(t + 1) * pad] = die_side[i * pad:(i + 1) * pad]
        for i in range(n):
            def store_int(g, a, value):
                back_send[i, at_rows(blk * 64 + g * 8, 16), lanes_of(a)] = value

            def store_die(g, a, value):
                die_back[i, at_rows(blk * 64 + g * 8, 16), lanes_of(a)] = value

            to_items(int_turn.at[i], pad, 8, store_int)
            to_items(die_turn.at[i], pad, 8, store_die)
        return carry

    lax.fori_loop(0, groups // 8, flux_step, 0)
    back_copies = []
    for d in range(1, n):
        peer = lax.rem(me_c + d, n)
        back_copies.append(send(back_send.at[peer], back_recv.at[me_c], back_sem, d, "chaos", peer))
    back_recv[me_c] = back_send[me_c]

    place = hot(iota((elem_rows, segs), 0) == die_row)

    def nodal(blk, own):
        to_tiles(lambda g, a: items[at_rows(blk * 48 + g * 8, 16), lanes_of(a)], 6, own, pad)
        both = jnp.concatenate([own[:4 * pad], own[4 * pad:]], axis=1).astype(bf16)
        return mm(both, back_sel)

    out_copies = []
    for d in range(1, n + 1):
        peer = lax.rem(me_c + d, n)
        items[...] = mm(place, die_back[peer])
        out_block = out_send.at[peer] if d < n else returned.at[me_c]

        def out_step(b, carry):
            for w in range(4):
                blk = 4 * b + w
                added = nodal(blk, turn.at[w])
                for u in range(4):
                    own = local_ref[blk * 4 + u, at_rows(peer * pad, pad), :] + added[u * pad:(u + 1) * pad]
                    q = (blk * 4 + u) // per
                    out_block[at_rows(q * high, high), lanes_of(u % per)] = own[:high].astype(bf16)
                    stage[q, :, lanes_of(u % per)] = own[high:]
            return carry

        lax.fori_loop(0, blocks // 4, out_step, 0)
        for q in range(16):
            tail_ref[q * low:(q + 1) * low, :] = stage[q, :low, :]
        out_block[16 * high:, :] = tail_ref[...].astype(bf16)

    finish(back_copies)
    for d in range(1, n):
        peer = lax.rem(me_c + d, n)
        out_copies.append(send(out_send.at[peer], returned.at[me_c], out_sem, d, "chaos", peer))
    everything = back_recv[...].reshape(n * segs, wide_lanes)
    spots = jnp.concatenate([share_out[i, ns:ns + 1, :] for i in range(n)], axis=1)
    slot_copies = []
    for d in range(1, ns + 1):
        peer = lax.rem(me_s + d, ns)
        found = mm(hot(iota((LANES, n * segs), 0) + peer * LANES == spots), everything).astype(bf16)
        if d < ns:
            back_slots[peer] = found
            slot_copies.append(send(back_slots.at[peer], back_got.at[me_s], back_slot_sem, d, "space", peer))
        else:
            back_got[me_s] = found
    finish(slot_copies)

    ids = jnp.concatenate([slot_ids(ask_out[s, 0:1, :], n, cap, faces) for s in range(ns)], axis=1)
    everything = back_got[...].reshape(ns * LANES, wide_lanes)
    summed = mm(hot(iota((n * faces, ns * LANES), 0) == ids), everything).astype(bf16)
    for i in range(n):
        code = share_out[i, ns + 1:ns + 2, :][:, :faces]
        items[...] = mm(hot(iota((elem_rows, faces), 0) == code), summed[i * faces:(i + 1) * faces])

        def delta_step(b, carry):
            for w in range(4):
                blk = 4 * b + w
                added = nodal(blk, turn.at[w])
                for u in range(4):
                    delta_ref[i * pairs + blk * 4 + u] = added[u * pad:(u + 1) * pad]
            return carry

        lax.fori_loop(0, blocks // 4, delta_step, 0)
    def place_out(block):
        tail_ref[...] = returned[block, 16 * high:, :].astype(f32)
        for q in range(16):
            for h in range(per):
                cols = pl.ds(pl.multiple_of(block * nodes + (q * per + h) * LANES, LANES), LANES)
                delta = delta_ref[block * pairs + q * per + h]
                upper = returned[block, q * high:(q + 1) * high, lanes_of(h)].astype(f32)
                out_ref[:high, cols] = (upper - delta[:high]).astype(bf16)
                lower = tail_ref[q * low:(q + 1) * low, lanes_of(h)]
                out_ref[high:part, cols] = (lower - delta[high:part]).astype(bf16)

    place_out(me_c)
    for d, copy in enumerate(out_copies, 1):
        copy.wait()
        place_out(lax.rem(me_c + n - d, n))


def local(
    field,
    stiffness,
    kl_coef,
    triple_mode,
    triple_row,
    triple_col,
    triple_value,
    die_elem,
    die_side,
    seg_owner,
    seg_face,
    die_mortar,
    int_mortar,
    bump_coef,
    int_elem,
    int_side,
):
    n, ns = lax.axis_size("chaos"), lax.axis_size("space")
    part, local_nodes = field.shape
    nodes = local_nodes // n
    segs = die_elem.shape[0]
    cap = max(2, 2 * segs // (n * ns))
    faces = int_elem.shape[0]
    pairs = nodes // LANES
    modes = bump_coef.shape[1] - 1
    high, low, pad = split_rows(part)
    rows = n * pad
    lanes = pad * FACE
    groups = segs // 8
    width = nodes // 16
    bf16, f32, i32 = jnp.bfloat16, jnp.float32, jnp.int32
    sel = face_select()

    height = (ns + 2 + 7) // 8 * 8
    packed = (n, 16 * part, width)

    def sems(count):
        return pltpu.SemaphoreType.DMA((2, count - 1))

    return pl.pallas_call(
        functools.partial(whole_kernel, n=n, ns=ns, cap=cap, faces=faces),
        out_shape=jax.ShapeDtypeStruct((part, local_nodes), bf16),
        in_specs=[pl.BlockSpec(memory_space=pltpu.VMEM)] * 18,
        out_specs=pl.BlockSpec(memory_space=pltpu.VMEM),
        scratch_shapes=(
            pltpu.VMEM((modes, rows, rows), bf16),
            pltpu.VMEM((pairs, rows, LANES), f32),
            pltpu.VMEM((groups, rows, LANES), bf16),
            pltpu.VMEM((n, segs, lanes), bf16),
            pltpu.VMEM((n, height, LANES), i32),
            pltpu.VMEM((ns, 8, LANES), i32),
            pltpu.VMEM((groups, LANES, LANES), bf16),
            pltpu.VMEM((groups, LANES, LANES), bf16),
            pltpu.VMEM((height, LANES), i32),
            pltpu.VMEM((ns, 8, LANES), i32),
            pltpu.VMEM(packed, bf16),
            pltpu.VMEM(packed, bf16),
            pltpu.VMEM((4, 4 * pad, LANES), bf16),
            pltpu.VMEM((n * pairs * 12, lanes), bf16),
            pltpu.VMEM((n * faces, lanes), bf16),
            pltpu.VMEM((ns, LANES, lanes), bf16),
            pltpu.VMEM((ns, LANES, lanes), bf16),
            pltpu.VMEM((n, segs, lanes), bf16),
            pltpu.VMEM((pairs, rows, LANES), bf16),
            pltpu.VMEM((2 * pairs * ELEM_NODES, LANES), f32),
            pltpu.VMEM((n, pairs * 12, lanes), bf16),
            pltpu.VMEM((pairs * 12, lanes), f32),
            pltpu.VMEM((max(n, 4), 8 * pad, LANES), f32),
            pltpu.VMEM((16 * low, width), f32),
            pltpu.VMEM((n, segs, lanes), bf16),
            pltpu.VMEM((n, segs, lanes), bf16),
            pltpu.VMEM((n, segs, lanes), bf16),
            pltpu.VMEM(packed, bf16),
            pltpu.VMEM(packed, bf16),
            pltpu.VMEM((ns, LANES, lanes), bf16),
            pltpu.VMEM((ns, LANES, lanes), bf16),
            pltpu.VMEM((n, 8 * pad, LANES), f32),
            pltpu.VMEM((n, 8 * pad, LANES), f32),
            pltpu.VMEM((16, 16, width), f32),
            pltpu.VMEM((n * pairs, pad, LANES), f32),
            sems(n), sems(ns), sems(n), sems(ns), sems(n), sems(n), sems(n), sems(ns),
        ),
        compiler_params=pltpu.CompilerParams(collective_id=0, has_side_effects=True, vmem_limit_bytes=VMEM_LIMIT),
        cost_estimate=pl.CostEstimate(flops=4 * modes * rows * rows * nodes, bytes_accessed=8 << 20, transcendentals=0),
    )(
        field, stiffness, kl_coef, triple_mode, triple_row, triple_col, triple_value, die_elem, die_side, seg_owner,
        seg_face, die_mortar, int_mortar, bump_coef, int_elem, int_side, sel, sel.T,
    )


def solution(mesh):
    in_specs = (
        P("chaos", "space"),
        P(("space", "chaos"), None),
        P(None, ("space", "chaos")),
        P(),
        P(),
        P(),
        P(),
        P(("space", "chaos")),
        P(("space", "chaos")),
        P(("space", "chaos")),
        P(("space", "chaos")),
        P(("space", "chaos"), None),
        P(("space", "chaos"), None),
        P(("space", "chaos"), None),
        P(("space", "chaos")),
        P(("space", "chaos")),
    )
    out_specs = P("chaos", "space")
    return jax.shard_map(local, mesh=mesh, in_specs=in_specs, out_specs=out_specs, check_vma=False)
```

```python
import functools

import jax
import jax.numpy as jnp
import numpy as np
from jax import lax
from jax.experimental import pallas as pl
from jax.experimental.pallas import tpu as pltpu
from jax.sharding import PartitionSpec as P

ELEM_NODES = 64
LANES = 128
FACE = 16
VMEM_LIMIT = 56 * 1024 * 1024
NT = (((1,), (1,)), ((), ()))
NN = (((1,), (0,)), ((), ()))
MESH = pl.DeviceIdType.MESH


def face_nodes():
    node_rows = []
    for side_idx in range(6):
        normal_axis = side_idx // 2
        plane_level = 3 * (side_idx % 2)
        row_nodes = []
        for first_coord in range(4):
            for second_coord in range(4):
                position = [first_coord, second_coord]
                position.insert(normal_axis, plane_level)
                row_nodes.append(16 * position[0] + 4 * position[1] + position[2])
        node_rows.append(row_nodes)
    return np.array(node_rows, dtype=np.int32)


def face_select():
    table = np.zeros((LANES, 2 * LANES), np.float32)
    for side, row in enumerate(face_nodes()):
        for point, node in enumerate(row):
            for half in range(2):
                table[half * ELEM_NODES + node, half * LANES + side * FACE + point] = 1.0
    return jnp.asarray(table, jnp.bfloat16)


def mm(a, b, dims=NN):
    return lax.dot_general(a, b, dims, preferred_element_type=jnp.float32)


def iota(shape, dim):
    return lax.broadcasted_iota(jnp.int32, shape, dim)


def hot(mask):
    return jnp.where(mask, 1.0, 0.0).astype(jnp.bfloat16)


def trade(x):
    group = iota((8, LANES), 1) // FACE
    for k in (1, 2, 4):
        upper = group // k % 2 == 1
        y = [None] * 8
        for v in range(8):
            if v & k:
                continue
            low, high = x[v], x[v + k]
            if high is not None:
                y[v] = jnp.where(upper, pltpu.roll(high, FACE * k, 1), low)
                y[v + k] = jnp.where(upper, high, pltpu.roll(low, LANES - FACE * k, 1))
            elif low is not None:
                y[v] = jnp.where(upper, 0.0, low)
                y[v + k] = jnp.where(upper, 0.0, pltpu.roll(low, LANES - FACE * k, 1))
        x = y
    return x


def to_items(turn, pad, count, store):
    for a in range(pad // 8):
        y = trade([turn[pl.ds(8 * a + b, 8, stride=pad), :] for b in range(8)])
        for g in range(0, count, 2):
            store(g, a, jnp.concatenate([y[g], y[g + 1]], axis=0).astype(jnp.bfloat16))


def to_tiles(load, count, turn, pad):
    for a in range(pad // 8):
        x = []
        for g in range(0, count, 2):
            both = load(g, a)
            x += [both[:8], both[8:]]
        y = trade(x + [None] * (8 - count))
        for b in range(8):
            turn[pl.ds(8 * a + b, 8, stride=pad), :] = y[b]


def face_row(elem, side):
    return lax.div(elem, 8) * 48 + side * 8 + lax.rem(elem, 2) * 4 + lax.div(lax.rem(elem, 8), 2)


def at_rows(start, count):
    return pl.ds(start if isinstance(start, int) else pl.multiple_of(start, 16), count)


def lanes_of(a):
    return slice(a * LANES, (a + 1) * LANES)


def column(row):
    size = row.shape[1]
    eye = iota((size, size), 0) == iota((size, size), 1)
    return jnp.sum(jnp.where(eye, row, 0), axis=1, keepdims=True)


def split_rows(part):
    high = part // 16 * 16
    return high, part - high, high + 16


def greet(axes):
    barrier = pltpu.get_barrier_semaphore()
    for axis, count in axes:
        me = lax.axis_index(axis)
        for d in range(1, count):
            pl.semaphore_signal(barrier, 1, device_id={axis: lax.rem(me + d, count)}, device_id_type=MESH)


def meet(axes):
    pl.semaphore_wait(pltpu.get_barrier_semaphore(), sum(count - 1 for _, count in axes))


def describe(src, dst, sems, d, axis, peer):
    return pltpu.make_async_remote_copy(
        src_ref=src, dst_ref=dst, send_sem=sems.at[0, d - 1], recv_sem=sems.at[1, d - 1],
        device_id={axis: peer}, device_id_type=MESH)


def send(*args):
    copy = describe(*args)
    copy.start()
    return copy


def finish(copies):
    for copy in copies:
        copy.wait()


def pack(load, store, tail_ref, part, width):
    high, low, _ = split_rows(part)
    for q in range(16):
        upper, lower = load(q)
        store(slice(q * high, (q + 1) * high), upper)
        tail_ref[q * low:(q + 1) * low, :] = lower.astype(jnp.float32)
    store(slice(16 * high, 16 * part), tail_ref[...].astype(jnp.bfloat16))


def mix(coupling_ref, block, weights):
    total = weights[0:1] * block.astype(jnp.float32)
    for k in range(coupling_ref.shape[0]):
        total = total + weights[k + 1:k + 2] * mm(coupling_ref[k], block)
    return total.astype(jnp.bfloat16)


def slot_ids(requests, n, cap, faces):
    lane = iota((1, LANES), 1)
    return lax.rem(lane // cap, n) * faces + requests


def row_of(ref):
    return ref[...].reshape(1, -1)


def whole_kernel(
    field_ref, stiff_ref, kl_ref, mode_ref, row_ref, col_ref, value_ref, die_elem_ref, die_side_ref, owner_ref,
    seg_face_ref, die_ref, int_ref, coef_ref, int_elem_ref, int_side_ref, sel_ref, back_sel_ref,
    out_ref,
    coupling_out, local_ref, proj_out, int_out, share_out, ask_out, die_diag, int_diag,
    msg, rows, sent, wide, block_ref, faces_ref, table_ref, slots, recv, picked, fp, stiff, die_faces, items, turn, tail_ref,
    back_send, back_recv, die_back, out_send, returned, back_slots, back_got, int_turn, die_turn, stage, delta_ref,
    share_sem, ask_sem, field_sem, slot_sem, pick_sem, back_sem, out_sem, back_slot_sem, *, n, ns, cap, faces,
):
    f32, bf16 = jnp.float32, jnp.bfloat16
    me_c, me_s = lax.axis_index("chaos"), lax.axis_index("space")
    axes = (("chaos", n), ("space", ns))
    greet(axes)
    part, local_nodes = field_ref.shape
    nodes = local_nodes // n
    width = nodes // 16
    per = width // LANES
    high, low, pad = split_rows(part)
    wide_lanes = pad * FACE
    modes, all_rows, _ = coupling_out.shape
    sel = sel_ref[...]

    owner, seg_face = row_of(owner_ref), row_of(seg_face_ref)
    die_row = face_row(row_of(die_elem_ref), row_of(die_side_ref))
    segs = owner.shape[1]
    r, c = iota((segs, segs), 0), iota((segs, segs), 1)
    owner_col, face_col = column(owner), column(seg_face)
    same = owner_col == owner
    rank_row = jnp.sum(jnp.where(same & (r < c), 1, 0), axis=0, keepdims=True)
    rank_col = jnp.sum(jnp.where(same & (c < r), 1, 0), axis=1, keepdims=True)
    base = me_c * (n * cap)
    lane_row = base + lax.rem(owner, n) * cap + rank_row
    lane_col = base + lax.rem(owner_col, n) * cap + rank_col
    left = hot(iota((16, segs), 0) == lax.div(owner, n))
    request = mm(left, jnp.where(c == lane_col, face_col, 0).astype(f32).astype(bf16))
    msg[...] = jnp.zeros(msg.shape, jnp.int32)
    msg[:ns, :] = request[:ns].astype(jnp.int32)
    msg[ns:ns + 1, :] = lax.div(owner, n) * LANES + lane_row
    msg[ns + 1:ns + 2, :faces] = face_row(row_of(int_elem_ref), row_of(int_side_ref))
    field_copies = []
    for d in range(1, n + 1):
        peer = lax.rem(me_c + d, n)
        start = peer * nodes

        def load(q):
            cols = pl.ds(pl.multiple_of(start + q * width, LANES), width)
            return field_ref[:high, cols], field_ref[high:part, cols]

        def store(where, value):
            if d < n:
                sent[peer, where, :] = value
            else:
                wide[me_c, where, :] = value

        pack(load, store, tail_ref, part, width)
        if d == 1:
            meet(axes)
            share_out[me_c] = msg[...]
            copies = [
                send(msg, share_out.at[me_c], share_sem, e, "chaos", lax.rem(me_c + e, n)) for e in range(1, n)
            ]
        if d < n:
            field_copies.append(send(sent.at[peer], wide.at[me_c], field_sem, d, "chaos", peer))
    finish(copies)

    total = share_out[0, :ns, :]
    for i in range(1, n):
        total = total + share_out[i, :ns, :]
    for s in range(ns):
        rows[s] = jnp.broadcast_to(total[s:s + 1, :], (8, LANES))
    ask_out[me_s] = rows[me_s]
    copies = []
    for d in range(1, ns):
        peer = lax.rem(me_s + d, ns)
        copies.append(send(rows.at[peer], ask_out.at[me_s], ask_sem, d, "space", peer))

    block_ref[...] = jnp.zeros(block_ref.shape, bf16)
    pairs = nodes // LANES
    blocks = pairs // 4

    def face_step(p, carry):
        for w in range(4):
            at = 4 * p + w
            for u in range(4):
                cols = pl.ds(pl.multiple_of((at * 4 + u) * LANES, LANES), LANES)
                block_ref[w, u * pad:u * pad + part, :] = field_ref[:, cols]
            found = mm(block_ref[w], sel)
            turn[w, :4 * pad] = found[:, :LANES]
            turn[w, 4 * pad:] = found[:, LANES:]

            def store(g, a, value):
                faces_ref[at_rows(at * 48 + g * 8, 16), lanes_of(a)] = value

            to_items(turn.at[w], pad, 6, store)
        return carry

    lax.fori_loop(0, n * blocks // 4, face_step, 0)
    elem_rows = blocks * 48
    for i in range(n):
        code = column(share_out[i, ns + 1:ns + 2, :])
        pick = hot(iota((LANES, elem_rows), 1) == code)
        found = mm(pick[:faces], faces_ref[i * elem_rows:(i + 1) * elem_rows, :])
        table_ref[i * faces:(i + 1) * faces, :] = found.astype(bf16)
    finish(copies)

    slot_copies = []
    for d in range(1, ns + 1):
        peer = lax.rem(me_s + d, ns)
        ids = column(slot_ids(ask_out[peer, 0:1, :], n, cap, faces))
        found = mm(hot(iota((LANES, n * faces), 1) == ids), table_ref[...]).astype(bf16)
        if d < ns:
            slots[peer] = found
            slot_copies.append(send(slots.at[peer], recv.at[me_s], slot_sem, d, "space", peer))
        else:
            recv[me_s] = found

    groups = die_diag.shape[0]
    lane_item = iota((FACE, LANES), 1) // FACE
    for mortar_ref, diag in ((die_ref, die_diag), (int_ref, int_diag)):
        for blk in range(groups // 8):
            for half in range(2):
                y = trade([
                    mortar_ref[blk * 64 + g // 2 * 16:blk * 64 + g // 2 * 16 + 16, lanes_of(half)].astype(f32)[
                        g % 2 * 8:g % 2 * 8 + 8] for g in range(8)
                ])
                for m in range(8):
                    turn[blk % 2, pl.ds(half * 8 + m, 8, stride=FACE), :] = y[m]
            for t in range(8):
                mat = turn[blk % 2, t * FACE:(t + 1) * FACE, :]
                for g in range(8):
                    diag[blk * 8 + t, g * FACE:(g + 1) * FACE, :] = jnp.where(lane_item == g, mat, 0.0).astype(bf16)

    def padded(chaos):
        return chaos + sum(jnp.where(chaos >= i * part, pad - part, 0) for i in range(1, n))

    value = row_of(value_ref)
    key = row_of(mode_ref) * all_rows + padded(row_of(row_ref))
    col = padded(row_of(col_ref))
    coarse = value.astype(bf16).astype(f32)
    at_col = iota((all_rows, key.shape[1]), 0) == col
    right = jnp.concatenate(
        [jnp.where(at_col, coarse, 0.0).astype(bf16), jnp.where(at_col, value - coarse, 0.0).astype(bf16)], axis=0
    )

    def mode_step(k, carry):
        at_row = hot(iota((all_rows, key.shape[1]), 0) + k * all_rows == key)
        both = mm(at_row, right, NT)
        coupling_out[k] = (both[:, :all_rows] + both[:, all_rows:]).astype(bf16)
        return carry

    lax.fori_loop(0, modes, mode_step, 0)

    elems = stiff_ref.shape[0]
    for t in range(ELEM_NODES // 2):
        block = stiff_ref[:, t * LANES:(t + 1) * LANES].astype(f32)
        stiff[pl.ds(2 * t, elems, stride=ELEM_NODES), :] = block
        stiff[pl.ds(2 * t + 1, elems, stride=ELEM_NODES), :] = pltpu.roll(block, ELEM_NODES, 1)

    finish(slot_copies)
    pick_copies = []
    everything = recv[...].reshape(ns * LANES, wide_lanes)
    for d in range(1, n + 1):
        peer = lax.rem(me_c + d, n)
        spot = column(share_out[peer, ns:ns + 1, :])
        found = mm(hot(iota((segs, ns * LANES), 1) == spot), everything).astype(bf16)
        if d < n:
            picked[peer] = found
            pick_copies.append(send(picked.at[peer], int_out.at[me_c], pick_sem, d, "chaos", peer))
        else:
            int_out[me_c] = found

    finish(field_copies)
    keep = iota((16, width), 0) < low
    for i in range(n):
        tail_ref[...] = wide[i, 16 * high:, :].astype(f32)
        for q in range(16):
            first = min(q * low, 16 * low - 16)
            tail = tail_ref[first:first + 16, :]
            if first < q * low:
                tail = pltpu.roll(tail, 16 - (q * low - first), 0)
            tail = jnp.where(keep, tail, 0.0).astype(bf16)
            for h in range(per):
                cols = slice(h * LANES, (h + 1) * LANES)
                fp[q * per + h, i * pad:i * pad + high, :] = wide[i, q * high:(q + 1) * high, cols]
                fp[q * per + h, i * pad + high:(i + 1) * pad, :] = tail[:, cols]

    lower = iota((ELEM_NODES, LANES), 1) < ELEM_NODES

    def element_step(p, carry):
        block = jnp.concatenate([fp[4 * p + u] for u in range(4)], axis=1)
        spread = jnp.where(iota((elems, 512), 1) // ELEM_NODES + 8 * p == iota((elems, 512), 0), 1.0, 0.0)
        weights = lax.dot_general(
            kl_ref[...], spread, NN, precision=lax.Precision.HIGHEST, preferred_element_type=f32)
        mixed = mix(coupling_out, block, weights)
        for h in range(4):
            at = pl.multiple_of((4 * p + h) * LANES, LANES)
            even = jnp.where(lower, stiff[pl.ds(at, ELEM_NODES), :], 0.0)
            odd = pltpu.roll(stiff[pl.ds(at + ELEM_NODES, ELEM_NODES), :], ELEM_NODES, 1)
            odd = jnp.where(lower, 0.0, odd)
            diag = jnp.concatenate([even, odd], axis=0).astype(bf16)
            local_ref[4 * p + h] = mm(mixed[:, lanes_of(h)], diag, NT)
        return carry

    def die_step(blk, carry):
        for u in range(4):
            found = mm(fp[4 * blk + u], sel)
            for i in range(n):
                for h in range(2):
                    turn[i, (4 * h + u) * pad:(4 * h + u + 1) * pad] = found[i * pad:(i + 1) * pad, lanes_of(h)]
        for d in range(1, n):
            i = lax.rem(me_c + d, n)

            def store(g, a, value):
                die_faces[i, at_rows(blk * 48 + g * 8, 16), lanes_of(a)] = value

            to_items(turn.at[i], pad, 6, store)
        return carry

    lax.fori_loop(0, blocks, die_step, 0)
    die_faces[me_c] = faces_ref[at_rows(me_c * elem_rows, elem_rows), :]
    pick = hot(iota((segs, elem_rows), 1) == column(die_row))
    for i in range(n):
        items[:segs] = mm(pick, die_faces[i])

        def project_step(blk, carry):
            to_tiles(lambda g, a: items[at_rows(blk * 64 + g * 8, 16), lanes_of(a)], 8, turn.at[0], pad)
            for t in range(8):
                proj_out[blk * 8 + t, i * pad:(i + 1) * pad, :] = turn[0, t * pad:(t + 1) * pad].astype(bf16)
            return carry

        lax.fori_loop(0, groups // 8, project_step, 0)

    def mortar_step(g, carry):
        proj_out[g] = mm(proj_out[g], die_diag[g], NT).astype(bf16)
        return carry

    lax.fori_loop(0, groups, mortar_step, 0, unroll=4)
    lax.fori_loop(0, pairs // 8, element_step, 0)
    finish(pick_copies)
    back_sel = back_sel_ref[...]

    def back_part(blk, d):
        own, peer = at_rows(blk * 64, 64), lax.rem(me_c + d, n)
        return back_send.at[peer, own], back_recv.at[me_c, own], back_sem, d + blk * (n - 1), "chaos", peer

    def flux_step(blk, carry):
        for i in range(n):
            to_tiles(
                lambda g, a: int_out[i, at_rows(blk * 64 + g * 8, 16), lanes_of(a)].astype(f32), 8, turn.at[i], pad)

        for r in range(2):
            jumps = []
            for h in range(4):
                t = 4 * r + h
                face = jnp.concatenate([turn[i, t * pad:(t + 1) * pad] for i in range(n)], axis=0).astype(bf16)
                own = mm(face, int_diag[blk * 8 + t], NT)
                jumps.append((proj_out[blk * 8 + t].astype(f32) - own).astype(bf16))
            lane = iota((segs, 512), 1)
            seg = blk * 64 + lane % LANES // FACE * 8 + 4 * r + lane // LANES
            weights = mm(coef_ref[...], hot(seg == iota((segs, 512), 0)))
            flux = mix(coupling_out, jnp.concatenate(jumps, axis=1), weights)
            for h in range(4):
                t = 4 * r + h
                own = flux[:, lanes_of(h)]
                int_side = mm(own, int_diag[blk * 8 + t])
                die_side = mm(own, die_diag[blk * 8 + t])
                for i in range(n):
                    int_turn[i, t * pad:(t + 1) * pad] = int_side[i * pad:(i + 1) * pad]
                    die_turn[i, t * pad:(t + 1) * pad] = die_side[i * pad:(i + 1) * pad]
        for i in range(n):
            def store_int(g, a, value):
                back_send[i, at_rows(blk * 64 + g * 8, 16), lanes_of(a)] = value

            def store_die(g, a, value):
                die_back[i, at_rows(blk * 64 + g * 8, 16), lanes_of(a)] = value

            to_items(int_turn.at[i], pad, 8, store_int)
            to_items(die_turn.at[i], pad, 8, store_die)
        for d in range(1, n):
            send(*back_part(blk, d))
        return carry

    lax.fori_loop(0, groups // 8, flux_step, 0)
    back_copies = [describe(*back_part(blk, d)) for blk in range(groups // 8) for d in range(1, n)]
    back_recv[me_c] = back_send[me_c]
    lax.fori_loop(pairs // 8, pairs // 4, element_step, 0)

    place = hot(iota((elem_rows, segs), 0) == die_row)

    def nodal(blk, own, size):
        to_tiles(lambda g, a: items[at_rows(blk * 48 + g * 8, 16), lanes_of(a)], 6, own, size)
        both = jnp.concatenate([own[:4 * size], own[4 * size:8 * size]], axis=1).astype(bf16)
        return mm(both, back_sel)

    out_copies = []
    for d in range(1, n + 1):
        peer = lax.rem(me_c + d, n)
        items[...] = mm(place, die_back[peer])
        out_block = out_send.at[peer] if d < n else returned.at[me_c]

        def out_step(b, carry):
            for w in range(4):
                blk = 4 * b + w
                added = nodal(blk, turn.at[w], pad)
                for u in range(4):
                    own = local_ref[blk * 4 + u, at_rows(peer * pad, pad), :] + added[u * pad:(u + 1) * pad]
                    q = (blk * 4 + u) // per
                    out_block[at_rows(q * high, high), lanes_of(u % per)] = own[:high].astype(bf16)
                    stage[q, :, lanes_of(u % per)] = own[high:]
            return carry

        lax.fori_loop(0, blocks // 4, out_step, 0)
        for q in range(16):
            tail_ref[q * low:(q + 1) * low, :] = stage[q, :low, :]
        out_block[16 * high:, :] = tail_ref[...].astype(bf16)

    finish(back_copies)
    for d in range(1, n):
        peer = lax.rem(me_c + d, n)
        out_copies.append(send(out_send.at[peer], returned.at[me_c], out_sem, d, "chaos", peer))
    everything = back_recv[...].reshape(n * segs, wide_lanes)
    spots = jnp.concatenate([share_out[i, ns:ns + 1, :] for i in range(n)], axis=1)
    size, half_lanes = pad, wide_lanes

    def fill(half):
        for d in range(1, ns + 1):
            peer = lax.rem(me_s + d, ns)
            place = hot(iota((LANES, n * segs), 0) + peer * LANES == spots)
            found = mm(place, everything[:, half * half_lanes:(half + 1) * half_lanes]).astype(bf16)
            if d < ns:
                back_slots[half, peer] = found
                if half == 0:
                    start(half, d, peer)
            else:
                back_got[half, me_s] = found

    half_copies = [[], []]

    def start(half, d, peer):
        half_copies[half].append(send(
            back_slots.at[half, peer], back_got.at[half, me_s], back_slot_sem, d + half * (ns - 1), "space", peer))

    ids = jnp.concatenate([slot_ids(ask_out[s, 0:1, :], n, cap, faces) for s in range(ns)], axis=1)

    def gather(half):
        got = back_got[half].reshape(ns * LANES, half_lanes)
        table_ref[:, :half_lanes] = mm(hot(iota((n * faces, ns * LANES), 0) == ids), got).astype(bf16)

        def gather_step(i, carry):
            code = share_out[i, ns + 1:ns + 2, :][:, :faces]
            items[:, :half_lanes] = mm(
                hot(iota((elem_rows, faces), 0) == code), table_ref[at_rows(i * faces, faces), :half_lanes])

            def delta_step(b, carry):
                for w in range(4):
                    blk = 4 * b + w
                    added = nodal(blk, turn.at[w], size)
                    for u in range(4):
                        delta_ref[i * pairs + blk * 4 + u, half * size:(half + 1) * size] = (
                            added[u * size:(u + 1) * size])
                return carry

            lax.fori_loop(0, blocks // 4, delta_step, 0)
            return carry

        lax.fori_loop(0, n, gather_step, 0)

    fill(0)
    finish(half_copies[0])
    gather(0)

    def place_out(block):
        tail_ref[...] = returned[block, 16 * high:, :].astype(f32)
        for q in range(16):
            for h in range(per):
                cols = pl.ds(pl.multiple_of(block * nodes + (q * per + h) * LANES, LANES), LANES)
                delta = delta_ref[block * pairs + q * per + h]
                upper = returned[block, q * high:(q + 1) * high, lanes_of(h)].astype(f32)
                out_ref[:high, cols] = (upper - delta[:high]).astype(bf16)
                lower = tail_ref[q * low:(q + 1) * low, lanes_of(h)]
                out_ref[high:part, cols] = (lower - delta[high:part]).astype(bf16)

    place_out(me_c)
    for d, copy in enumerate(out_copies, 1):
        copy.wait()
        place_out(lax.rem(me_c + n - d, n))


def local(
    field,
    stiffness,
    kl_coef,
    triple_mode,
    triple_row,
    triple_col,
    triple_value,
    die_elem,
    die_side,
    seg_owner,
    seg_face,
    die_mortar,
    int_mortar,
    bump_coef,
    int_elem,
    int_side,
):
    n, ns = lax.axis_size("chaos"), lax.axis_size("space")
    part, local_nodes = field.shape
    nodes = local_nodes // n
    segs = die_elem.shape[0]
    cap = max(2, 2 * segs // (n * ns))
    faces = int_elem.shape[0]
    pairs = nodes // LANES
    modes = bump_coef.shape[1] - 1
    high, low, pad = split_rows(part)
    rows = n * pad
    lanes = pad * FACE
    groups = segs // 8
    width = nodes // 16
    bf16, f32, i32 = jnp.bfloat16, jnp.float32, jnp.int32
    sel = face_select()

    height = (ns + 2 + 7) // 8 * 8
    packed = (n, 16 * part, width)

    def sems(count, rounds=1):
        return pltpu.SemaphoreType.DMA((2, rounds * (count - 1)))

    return pl.pallas_call(
        functools.partial(whole_kernel, n=n, ns=ns, cap=cap, faces=faces),
        out_shape=jax.ShapeDtypeStruct((part, local_nodes), bf16),
        in_specs=[pl.BlockSpec(memory_space=pltpu.VMEM)] * 18,
        out_specs=pl.BlockSpec(memory_space=pltpu.VMEM),
        scratch_shapes=(
            pltpu.VMEM((modes, rows, rows), bf16),
            pltpu.VMEM((pairs, rows, LANES), f32),
            pltpu.VMEM((groups, rows, LANES), bf16),
            pltpu.VMEM((n, segs, lanes), bf16),
            pltpu.VMEM((n, height, LANES), i32),
            pltpu.VMEM((ns, 8, LANES), i32),
            pltpu.VMEM((groups, LANES, LANES), bf16),
            pltpu.VMEM((groups, LANES, LANES), bf16),
            pltpu.VMEM((height, LANES), i32),
            pltpu.VMEM((ns, 8, LANES), i32),
            pltpu.VMEM(packed, bf16),
            pltpu.VMEM(packed, bf16),
            pltpu.VMEM((4, 4 * pad, LANES), bf16),
            pltpu.VMEM((n * pairs * 12, lanes), bf16),
            pltpu.VMEM((n * faces, lanes), bf16),
            pltpu.VMEM((ns, LANES, lanes), bf16),
            pltpu.VMEM((ns, LANES, lanes), bf16),
            pltpu.VMEM((n, segs, lanes), bf16),
            pltpu.VMEM((pairs, rows, LANES), bf16),
            pltpu.VMEM((2 * pairs * ELEM_NODES, LANES), f32),
            pltpu.VMEM((n, pairs * 12, lanes), bf16),
            pltpu.VMEM((pairs * 12, lanes), f32),
            pltpu.VMEM((max(n, 4), 8 * pad, LANES), f32),
            pltpu.VMEM((16 * low, width), f32),
            pltpu.VMEM((n, segs, lanes), bf16),
            pltpu.VMEM((n, segs, lanes), bf16),
            pltpu.VMEM((n, segs, lanes), bf16),
            pltpu.VMEM(packed, bf16),
            pltpu.VMEM(packed, bf16),
            pltpu.VMEM((1, ns, LANES, lanes), bf16),
            pltpu.VMEM((1, ns, LANES, lanes), bf16),
            pltpu.VMEM((n, 8 * pad, LANES), f32),
            pltpu.VMEM((n, 8 * pad, LANES), f32),
            pltpu.VMEM((16, 16, width), f32),
            pltpu.VMEM((n * pairs, pad, LANES), f32),
            sems(n), sems(ns), sems(n), sems(ns), sems(n), sems(n, groups // 8), sems(n), sems(ns),
        ),
        compiler_params=pltpu.CompilerParams(collective_id=0, has_side_effects=True, vmem_limit_bytes=VMEM_LIMIT),
        cost_estimate=pl.CostEstimate(flops=4 * modes * rows * rows * nodes, bytes_accessed=8 << 20, transcendentals=0),
    )(
        field, stiffness, kl_coef, triple_mode, triple_row, triple_col, triple_value, die_elem, die_side, seg_owner,
        seg_face, die_mortar, int_mortar, bump_coef.T, int_elem, int_side, sel, sel.T,
    )


def solution(mesh):
    in_specs = (
        P("chaos", "space"),
        P(("space", "chaos"), None),
        P(None, ("space", "chaos")),
        P(),
        P(),
        P(),
        P(),
        P(("space", "chaos")),
        P(("space", "chaos")),
        P(("space", "chaos")),
        P(("space", "chaos")),
        P(("space", "chaos"), None),
        P(("space", "chaos"), None),
        P(("space", "chaos"), None),
        P(("space", "chaos")),
        P(("space", "chaos")),
    )
    out_specs = P("chaos", "space")
    return jax.shard_map(local, mesh=mesh, in_specs=in_specs, out_specs=out_specs, check_vma=False)
```

```python
import functools

import jax
import jax.numpy as jnp
import numpy as np
from jax import lax
from jax.experimental import pallas as pl
from jax.experimental.pallas import tpu as pltpu
from jax.sharding import PartitionSpec as P

ELEM_NODES = 64
LANES = 128
FACE = 16
VMEM_LIMIT = 56 * 1024 * 1024
NT = (((1,), (1,)), ((), ()))
NN = (((1,), (0,)), ((), ()))
MESH = pl.DeviceIdType.MESH


def face_nodes():
    node_rows = []
    for side_idx in range(6):
        normal_axis = side_idx // 2
        plane_level = 3 * (side_idx % 2)
        row_nodes = []
        for first_coord in range(4):
            for second_coord in range(4):
                position = [first_coord, second_coord]
                position.insert(normal_axis, plane_level)
                row_nodes.append(16 * position[0] + 4 * position[1] + position[2])
        node_rows.append(row_nodes)
    return np.array(node_rows, dtype=np.int32)


def face_select():
    table = np.zeros((LANES, 2 * LANES), np.float32)
    for side, row in enumerate(face_nodes()):
        for point, node in enumerate(row):
            for half in range(2):
                table[half * ELEM_NODES + node, half * LANES + side * FACE + point] = 1.0
    return jnp.asarray(table, jnp.bfloat16)


def mm(a, b, dims=NN):
    return lax.dot_general(a, b, dims, preferred_element_type=jnp.float32)


def iota(shape, dim):
    return lax.broadcasted_iota(jnp.int32, shape, dim)


def hot(mask):
    return jnp.where(mask, 1.0, 0.0).astype(jnp.bfloat16)


def trade(x):
    group = iota((8, LANES), 1) // FACE
    for k in (1, 2, 4):
        upper = group // k % 2 == 1
        y = [None] * 8
        for v in range(8):
            if v & k:
                continue
            low, high = x[v], x[v + k]
            if high is not None:
                y[v] = jnp.where(upper, pltpu.roll(high, FACE * k, 1), low)
                y[v + k] = jnp.where(upper, high, pltpu.roll(low, LANES - FACE * k, 1))
            elif low is not None:
                y[v] = jnp.where(upper, 0.0, low)
                y[v + k] = jnp.where(upper, 0.0, pltpu.roll(low, LANES - FACE * k, 1))
        x = y
    return x


def to_items(turn, pad, count, store):
    for a in range(pad // 8):
        y = trade([turn[pl.ds(8 * a + b, 8, stride=pad), :] for b in range(8)])
        for g in range(0, count, 2):
            store(g, a, jnp.concatenate([y[g], y[g + 1]], axis=0).astype(jnp.bfloat16))


def to_tiles(load, count, turn, pad):
    for a in range(pad // 8):
        x = []
        for g in range(0, count, 2):
            both = load(g, a)
            x += [both[:8], both[8:]]
        y = trade(x + [None] * (8 - count))
        for b in range(8):
            turn[pl.ds(8 * a + b, 8, stride=pad), :] = y[b]


def face_row(elem, side):
    return lax.div(elem, 8) * 48 + side * 8 + lax.rem(elem, 2) * 4 + lax.div(lax.rem(elem, 8), 2)


def at_rows(start, count):
    return pl.ds(start if isinstance(start, int) else pl.multiple_of(start, 16), count)


def lanes_of(a):
    return slice(a * LANES, (a + 1) * LANES)


def column(row):
    size = row.shape[1]
    eye = iota((size, size), 0) == iota((size, size), 1)
    return jnp.sum(jnp.where(eye, row, 0), axis=1, keepdims=True)


def split_rows(part):
    high = part // 16 * 16
    return high, part - high, high + 16


def greet(axes):
    barrier = pltpu.get_barrier_semaphore()
    for axis, count in axes:
        me = lax.axis_index(axis)
        for d in range(1, count):
            pl.semaphore_signal(barrier, 1, device_id={axis: lax.rem(me + d, count)}, device_id_type=MESH)


def meet(axes):
    pl.semaphore_wait(pltpu.get_barrier_semaphore(), sum(count - 1 for _, count in axes))


def describe(src, dst, sems, d, axis, peer):
    return pltpu.make_async_remote_copy(
        src_ref=src, dst_ref=dst, send_sem=sems.at[0, d - 1], recv_sem=sems.at[1, d - 1],
        device_id={axis: peer}, device_id_type=MESH)


def send(*args):
    copy = describe(*args)
    copy.start()
    return copy


def finish(copies):
    for copy in copies:
        copy.wait()


def pack(load, store, tail_ref, part, width):
    high, low, _ = split_rows(part)
    for q in range(16):
        upper, lower = load(q)
        store(slice(q * high, (q + 1) * high), upper)
        tail_ref[q * low:(q + 1) * low, :] = lower.astype(jnp.float32)
    store(slice(16 * high, 16 * part), tail_ref[...].astype(jnp.bfloat16))


def mix(coupling_ref, block, weights):
    total = weights[0:1] * block.astype(jnp.float32)
    for k in range(coupling_ref.shape[0]):
        total = total + weights[k + 1:k + 2] * mm(coupling_ref[k], block)
    return total.astype(jnp.bfloat16)


def slot_ids(requests, n, cap, faces):
    lane = iota((1, LANES), 1)
    return lax.rem(lane // cap, n) * faces + requests


def row_of(ref):
    return ref[...].reshape(1, -1)


def whole_kernel(
    field_ref, stiff_ref, kl_ref, mode_ref, row_ref, col_ref, value_ref, die_elem_ref, die_side_ref, owner_ref,
    seg_face_ref, die_ref, int_ref, coef_ref, int_elem_ref, int_side_ref, sel_ref, back_sel_ref,
    out_ref,
    coupling_out, local_ref, proj_out, int_out, share_out, ask_out, die_diag, int_diag,
    msg, rows, sent, wide, block_ref, faces_ref, table_ref, slots, recv, picked, fp, stiff, die_faces, items, turn, tail_ref,
    back_send, back_recv, die_back, out_send, returned, back_slots, back_got, int_turn, die_turn, stage, delta_ref,
    share_sem, ask_sem, field_sem, slot_sem, pick_sem, back_sem, out_sem, back_slot_sem, *, n, ns, cap, faces,
):
    f32, bf16 = jnp.float32, jnp.bfloat16
    me_c, me_s = lax.axis_index("chaos"), lax.axis_index("space")
    axes = (("chaos", n), ("space", ns))
    greet(axes)
    part, local_nodes = field_ref.shape
    nodes = local_nodes // n
    width = nodes // 16
    per = width // LANES
    high, low, pad = split_rows(part)
    wide_lanes = pad * FACE
    modes, all_rows, _ = coupling_out.shape
    sel = sel_ref[...]

    owner, seg_face = row_of(owner_ref), row_of(seg_face_ref)
    die_row = face_row(row_of(die_elem_ref), row_of(die_side_ref))
    segs = owner.shape[1]
    r, c = iota((segs, segs), 0), iota((segs, segs), 1)
    owner_col, face_col = column(owner), column(seg_face)
    same = owner_col == owner
    rank_row = jnp.sum(jnp.where(same & (r < c), 1, 0), axis=0, keepdims=True)
    rank_col = jnp.sum(jnp.where(same & (c < r), 1, 0), axis=1, keepdims=True)
    base = me_c * (n * cap)
    lane_row = base + lax.rem(owner, n) * cap + rank_row
    lane_col = base + lax.rem(owner_col, n) * cap + rank_col
    left = hot(iota((16, segs), 0) == lax.div(owner, n))
    request = mm(left, jnp.where(c == lane_col, face_col, 0).astype(f32).astype(bf16))
    msg[...] = jnp.zeros(msg.shape, jnp.int32)
    msg[:ns, :] = request[:ns].astype(jnp.int32)
    msg[ns:ns + 1, :] = lax.div(owner, n) * LANES + lane_row
    msg[ns + 1:ns + 2, :faces] = face_row(row_of(int_elem_ref), row_of(int_side_ref))
    field_copies = []
    for d in range(1, n + 1):
        peer = lax.rem(me_c + d, n)
        start = peer * nodes

        def load(q):
            cols = pl.ds(pl.multiple_of(start + q * width, LANES), width)
            return field_ref[:high, cols], field_ref[high:part, cols]

        def store(where, value):
            if d < n:
                sent[peer, where, :] = value
            else:
                wide[me_c, where, :] = value

        pack(load, store, tail_ref, part, width)
        if d == 1:
            meet(axes)
            share_out[me_c] = msg[...]
            copies = [
                send(msg, share_out.at[me_c], share_sem, e, "chaos", lax.rem(me_c + e, n)) for e in range(1, n)
            ]
        if d < n:
            field_copies.append(send(sent.at[peer], wide.at[me_c], field_sem, d, "chaos", peer))
    finish(copies)

    total = share_out[0, :ns, :]
    for i in range(1, n):
        total = total + share_out[i, :ns, :]
    for s in range(ns):
        rows[s] = jnp.broadcast_to(total[s:s + 1, :], (8, LANES))
    ask_out[me_s] = rows[me_s]
    copies = []
    for d in range(1, ns):
        peer = lax.rem(me_s + d, ns)
        copies.append(send(rows.at[peer], ask_out.at[me_s], ask_sem, d, "space", peer))

    block_ref[...] = jnp.zeros(block_ref.shape, bf16)
    pairs = nodes // LANES
    blocks = pairs // 4

    def face_step(p, carry):
        for w in range(4):
            at = 4 * p + w
            for u in range(4):
                cols = pl.ds(pl.multiple_of((at * 4 + u) * LANES, LANES), LANES)
                block_ref[w, u * pad:u * pad + part, :] = field_ref[:, cols]
            found = mm(block_ref[w], sel)
            turn[w, :4 * pad] = found[:, :LANES]
            turn[w, 4 * pad:] = found[:, LANES:]

            def store(g, a, value):
                faces_ref[at_rows(at * 48 + g * 8, 16), lanes_of(a)] = value

            to_items(turn.at[w], pad, 6, store)
        return carry

    lax.fori_loop(0, n * blocks // 4, face_step, 0)
    elem_rows = blocks * 48
    for i in range(n):
        code = column(share_out[i, ns + 1:ns + 2, :])
        pick = hot(iota((LANES, elem_rows), 1) == code)
        found = mm(pick[:faces], faces_ref[i * elem_rows:(i + 1) * elem_rows, :])
        table_ref[i * faces:(i + 1) * faces, :] = found.astype(bf16)
    finish(copies)

    slot_copies = []
    for d in range(1, ns + 1):
        peer = lax.rem(me_s + d, ns)
        ids = column(slot_ids(ask_out[peer, 0:1, :], n, cap, faces))
        found = mm(hot(iota((LANES, n * faces), 1) == ids), table_ref[...]).astype(bf16)
        if d < ns:
            slots[peer] = found
            slot_copies.append(send(slots.at[peer], recv.at[me_s], slot_sem, d, "space", peer))
        else:
            recv[me_s] = found

    groups = die_diag.shape[0]
    lane_item = iota((FACE, LANES), 1) // FACE
    for mortar_ref, diag in ((die_ref, die_diag), (int_ref, int_diag)):
        for blk in range(groups // 8):
            for half in range(2):
                y = trade([
                    mortar_ref[blk * 64 + g // 2 * 16:blk * 64 + g // 2 * 16 + 16, lanes_of(half)].astype(f32)[
                        g % 2 * 8:g % 2 * 8 + 8] for g in range(8)
                ])
                for m in range(8):
                    turn[blk % 2, pl.ds(half * 8 + m, 8, stride=FACE), :] = y[m]
            for t in range(8):
                mat = turn[blk % 2, t * FACE:(t + 1) * FACE, :]
                for g in range(8):
                    diag[blk * 8 + t, g * FACE:(g + 1) * FACE, :] = jnp.where(lane_item == g, mat, 0.0).astype(bf16)

    def padded(chaos):
        return chaos + sum(jnp.where(chaos >= i * part, pad - part, 0) for i in range(1, n))

    value = row_of(value_ref)
    key = row_of(mode_ref) * all_rows + padded(row_of(row_ref))
    col = padded(row_of(col_ref))
    coarse = value.astype(bf16).astype(f32)
    at_col = iota((all_rows, key.shape[1]), 0) == col
    right = jnp.concatenate(
        [jnp.where(at_col, coarse, 0.0).astype(bf16), jnp.where(at_col, value - coarse, 0.0).astype(bf16)], axis=0
    )

    def mode_step(k, carry):
        at_row = hot(iota((all_rows, key.shape[1]), 0) + k * all_rows == key)
        both = mm(at_row, right, NT)
        coupling_out[k] = (both[:, :all_rows] + both[:, all_rows:]).astype(bf16)
        return carry

    lax.fori_loop(0, modes, mode_step, 0)

    elems = stiff_ref.shape[0]
    for t in range(ELEM_NODES // 2):
        block = stiff_ref[:, t * LANES:(t + 1) * LANES].astype(f32)
        stiff[pl.ds(2 * t, elems, stride=ELEM_NODES), :] = block
        stiff[pl.ds(2 * t + 1, elems, stride=ELEM_NODES), :] = pltpu.roll(block, ELEM_NODES, 1)

    finish(slot_copies)
    pick_copies = []
    everything = recv[...].reshape(ns * LANES, wide_lanes)
    for d in range(1, n + 1):
        peer = lax.rem(me_c + d, n)
        spot = column(share_out[peer, ns:ns + 1, :])
        found = mm(hot(iota((segs, ns * LANES), 1) == spot), everything).astype(bf16)
        if d < n:
            picked[peer] = found
            pick_copies.append(send(picked.at[peer], int_out.at[me_c], pick_sem, d, "chaos", peer))
        else:
            int_out[me_c] = found

    finish(field_copies)
    keep = iota((16, width), 0) < low
    for i in range(n):
        tail_ref[...] = wide[i, 16 * high:, :].astype(f32)
        for q in range(16):
            first = min(q * low, 16 * low - 16)
            tail = tail_ref[first:first + 16, :]
            if first < q * low:
                tail = pltpu.roll(tail, 16 - (q * low - first), 0)
            tail = jnp.where(keep, tail, 0.0).astype(bf16)
            for h in range(per):
                cols = slice(h * LANES, (h + 1) * LANES)
                fp[q * per + h, i * pad:i * pad + high, :] = wide[i, q * high:(q + 1) * high, cols]
                fp[q * per + h, i * pad + high:(i + 1) * pad, :] = tail[:, cols]

    lower = iota((ELEM_NODES, LANES), 1) < ELEM_NODES

    def element_step(p, carry):
        block = jnp.concatenate([fp[4 * p + u] for u in range(4)], axis=1)
        spread = jnp.where(iota((elems, 512), 1) // ELEM_NODES + 8 * p == iota((elems, 512), 0), 1.0, 0.0)
        weights = lax.dot_general(
            kl_ref[...], spread, NN, precision=lax.Precision.HIGHEST, preferred_element_type=f32)
        mixed = mix(coupling_out, block, weights)
        for h in range(4):
            at = pl.multiple_of((4 * p + h) * LANES, LANES)
            even = jnp.where(lower, stiff[pl.ds(at, ELEM_NODES), :], 0.0)
            odd = pltpu.roll(stiff[pl.ds(at + ELEM_NODES, ELEM_NODES), :], ELEM_NODES, 1)
            odd = jnp.where(lower, 0.0, odd)
            diag = jnp.concatenate([even, odd], axis=0).astype(bf16)
            local_ref[4 * p + h] = mm(mixed[:, lanes_of(h)], diag, NT)
        return carry

    def die_step(blk, carry):
        for u in range(4):
            found = mm(fp[4 * blk + u], sel)
            for i in range(n):
                for h in range(2):
                    turn[i, (4 * h + u) * pad:(4 * h + u + 1) * pad] = found[i * pad:(i + 1) * pad, lanes_of(h)]
        for d in range(1, n):
            i = lax.rem(me_c + d, n)

            def store(g, a, value):
                die_faces[i, at_rows(blk * 48 + g * 8, 16), lanes_of(a)] = value

            to_items(turn.at[i], pad, 6, store)
        return carry

    lax.fori_loop(0, blocks, die_step, 0)
    die_faces[me_c] = faces_ref[at_rows(me_c * elem_rows, elem_rows), :]
    pick = hot(iota((segs, elem_rows), 1) == column(die_row))
    for i in range(n):
        items[:segs] = mm(pick, die_faces[i])

        def project_step(blk, carry):
            to_tiles(lambda g, a: items[at_rows(blk * 64 + g * 8, 16), lanes_of(a)], 8, turn.at[0], pad)
            for t in range(8):
                proj_out[blk * 8 + t, i * pad:(i + 1) * pad, :] = turn[0, t * pad:(t + 1) * pad].astype(bf16)
            return carry

        lax.fori_loop(0, groups // 8, project_step, 0)

    def mortar_step(g, carry):
        proj_out[g] = mm(proj_out[g], die_diag[g], NT).astype(bf16)
        return carry

    lax.fori_loop(0, groups, mortar_step, 0, unroll=4)
    lax.fori_loop(0, pairs // 8, element_step, 0)
    finish(pick_copies)
    back_sel = back_sel_ref[...]

    def back_part(blk, d):
        own, peer = at_rows(blk * 64, 64), lax.rem(me_c + d, n)
        return back_send.at[peer, own], back_recv.at[me_c, own], back_sem, d + blk * (n - 1), "chaos", peer

    def flux_step(blk, carry):
        for i in range(n):
            to_tiles(
                lambda g, a: int_out[i, at_rows(blk * 64 + g * 8, 16), lanes_of(a)].astype(f32), 8, turn.at[i], pad)

        for r in range(2):
            jumps = []
            for h in range(4):
                t = 4 * r + h
                face = jnp.concatenate([turn[i, t * pad:(t + 1) * pad] for i in range(n)], axis=0).astype(bf16)
                own = mm(face, int_diag[blk * 8 + t], NT)
                jumps.append((proj_out[blk * 8 + t].astype(f32) - own).astype(bf16))
            lane = iota((segs, 512), 1)
            seg = blk * 64 + lane % LANES // FACE * 8 + 4 * r + lane // LANES
            weights = mm(coef_ref[...], hot(seg == iota((segs, 512), 0)))
            flux = mix(coupling_out, jnp.concatenate(jumps, axis=1), weights)
            for h in range(4):
                t = 4 * r + h
                own = flux[:, lanes_of(h)]
                int_side = mm(own, int_diag[blk * 8 + t])
                die_side = mm(own, die_diag[blk * 8 + t])
                for i in range(n):
                    int_turn[i, t * pad:(t + 1) * pad] = int_side[i * pad:(i + 1) * pad]
                    die_turn[i, t * pad:(t + 1) * pad] = die_side[i * pad:(i + 1) * pad]
        for i in range(n):
            def store_int(g, a, value):
                back_send[i, at_rows(blk * 64 + g * 8, 16), lanes_of(a)] = value

            def store_die(g, a, value):
                die_back[i, at_rows(blk * 64 + g * 8, 16), lanes_of(a)] = value

            to_items(int_turn.at[i], pad, 8, store_int)
            to_items(die_turn.at[i], pad, 8, store_die)
        for d in range(1, n):
            send(*back_part(blk, d))
        return carry

    lax.fori_loop(0, groups // 8, flux_step, 0)
    back_copies = [describe(*back_part(blk, d)) for blk in range(groups // 8) for d in range(1, n)]
    back_recv[me_c] = back_send[me_c]
    lax.fori_loop(pairs // 8, pairs // 4, element_step, 0)

    place = hot(iota((elem_rows, segs), 0) == die_row)

    def nodal(blk, own, size):
        to_tiles(lambda g, a: items[at_rows(blk * 48 + g * 8, 16), lanes_of(a)], 6, own, size)
        both = jnp.concatenate([own[:4 * size], own[4 * size:8 * size]], axis=1).astype(bf16)
        return mm(both, back_sel)

    out_copies = []
    for d in range(1, n + 1):
        peer = lax.rem(me_c + d, n)
        items[...] = mm(place, die_back[peer])
        out_block = out_send.at[peer] if d < n else returned.at[me_c]

        def out_step(b, carry):
            for w in range(4):
                blk = 4 * b + w
                added = nodal(blk, turn.at[w], pad)
                for u in range(4):
                    own = local_ref[blk * 4 + u, at_rows(peer * pad, pad), :] + added[u * pad:(u + 1) * pad]
                    q = (blk * 4 + u) // per
                    out_block[at_rows(q * high, high), lanes_of(u % per)] = own[:high].astype(bf16)
                    stage[q, :, lanes_of(u % per)] = own[high:]
            return carry

        lax.fori_loop(0, blocks // 4, out_step, 0)
        for q in range(16):
            tail_ref[q * low:(q + 1) * low, :] = stage[q, :low, :]
        out_block[16 * high:, :] = tail_ref[...].astype(bf16)

    finish(back_copies)
    for d in range(1, n):
        peer = lax.rem(me_c + d, n)
        out_copies.append(send(out_send.at[peer], returned.at[me_c], out_sem, d, "chaos", peer))
    everything = back_recv[...].reshape(n * segs, wide_lanes)
    spots = jnp.concatenate([share_out[i, ns:ns + 1, :] for i in range(n)], axis=1)
    size, half_lanes = pad, wide_lanes

    def fill(half):
        for d in range(1, ns + 1):
            peer = lax.rem(me_s + d, ns)
            place = hot(iota((LANES, n * segs), 0) + peer * LANES == spots)
            found = mm(place, everything[:, half * half_lanes:(half + 1) * half_lanes]).astype(bf16)
            if d < ns:
                back_slots[half, peer] = found
                if half == 0:
                    start(half, d, peer)
            else:
                back_got[half, me_s] = found

    half_copies = [[], []]

    def start(half, d, peer):
        half_copies[half].append(send(
            back_slots.at[half, peer], back_got.at[half, me_s], back_slot_sem, d + half * (ns - 1), "space", peer))

    ids = jnp.concatenate([slot_ids(ask_out[s, 0:1, :], n, cap, faces) for s in range(ns)], axis=1)

    def gather(half):
        got = back_got[half].reshape(ns * LANES, half_lanes)
        table_ref[:, :half_lanes] = mm(hot(iota((n * faces, ns * LANES), 0) == ids), got).astype(bf16)

        def gather_step(i, carry):
            code = share_out[i, ns + 1:ns + 2, :][:, :faces]
            items[:, :half_lanes] = mm(
                hot(iota((elem_rows, faces), 0) == code), table_ref[at_rows(i * faces, faces), :half_lanes])

            def delta_step(b, carry):
                for w in range(8):
                    blk = 8 * b + w
                    added = nodal(blk, turn.at[w] if w < 4 else int_turn.at[w - 4], size)
                    for u in range(4):
                        delta_ref[i * pairs + blk * 4 + u, half * size:(half + 1) * size] = (
                            added[u * size:(u + 1) * size])
                return carry

            lax.fori_loop(0, blocks // 8, delta_step, 0)
            return carry

        lax.fori_loop(0, n, gather_step, 0)

    fill(0)
    finish(half_copies[0])
    gather(0)

    def place_out(block):
        tail_ref[...] = returned[block, 16 * high:, :].astype(f32)
        for q in range(16):
            for h in range(per):
                cols = pl.ds(pl.multiple_of(block * nodes + (q * per + h) * LANES, LANES), LANES)
                delta = delta_ref[block * pairs + q * per + h]
                upper = returned[block, q * high:(q + 1) * high, lanes_of(h)].astype(f32)
                out_ref[:high, cols] = (upper - delta[:high]).astype(bf16)
                lower = tail_ref[q * low:(q + 1) * low, lanes_of(h)]
                out_ref[high:part, cols] = (lower - delta[high:part]).astype(bf16)

    place_out(me_c)
    for d, copy in enumerate(out_copies, 1):
        copy.wait()
        place_out(lax.rem(me_c + n - d, n))


def local(
    field,
    stiffness,
    kl_coef,
    triple_mode,
    triple_row,
    triple_col,
    triple_value,
    die_elem,
    die_side,
    seg_owner,
    seg_face,
    die_mortar,
    int_mortar,
    bump_coef,
    int_elem,
    int_side,
):
    n, ns = lax.axis_size("chaos"), lax.axis_size("space")
    part, local_nodes = field.shape
    nodes = local_nodes // n
    segs = die_elem.shape[0]
    cap = max(2, 2 * segs // (n * ns))
    faces = int_elem.shape[0]
    pairs = nodes // LANES
    modes = bump_coef.shape[1] - 1
    high, low, pad = split_rows(part)
    rows = n * pad
    lanes = pad * FACE
    groups = segs // 8
    width = nodes // 16
    bf16, f32, i32 = jnp.bfloat16, jnp.float32, jnp.int32
    sel = face_select()

    height = (ns + 2 + 7) // 8 * 8
    packed = (n, 16 * part, width)

    def sems(count, rounds=1):
        return pltpu.SemaphoreType.DMA((2, rounds * (count - 1)))

    return pl.pallas_call(
        functools.partial(whole_kernel, n=n, ns=ns, cap=cap, faces=faces),
        out_shape=jax.ShapeDtypeStruct((part, local_nodes), bf16),
        in_specs=[pl.BlockSpec(memory_space=pltpu.VMEM)] * 18,
        out_specs=pl.BlockSpec(memory_space=pltpu.VMEM),
        scratch_shapes=(
            pltpu.VMEM((modes, rows, rows), bf16),
            pltpu.VMEM((pairs, rows, LANES), f32),
            pltpu.VMEM((groups, rows, LANES), bf16),
            pltpu.VMEM((n, segs, lanes), bf16),
            pltpu.VMEM((n, height, LANES), i32),
            pltpu.VMEM((ns, 8, LANES), i32),
            pltpu.VMEM((groups, LANES, LANES), bf16),
            pltpu.VMEM((groups, LANES, LANES), bf16),
            pltpu.VMEM((height, LANES), i32),
            pltpu.VMEM((ns, 8, LANES), i32),
            pltpu.VMEM(packed, bf16),
            pltpu.VMEM(packed, bf16),
            pltpu.VMEM((4, 4 * pad, LANES), bf16),
            pltpu.VMEM((n * pairs * 12, lanes), bf16),
            pltpu.VMEM((n * faces, lanes), bf16),
            pltpu.VMEM((ns, LANES, lanes), bf16),
            pltpu.VMEM((ns, LANES, lanes), bf16),
            pltpu.VMEM((n, segs, lanes), bf16),
            pltpu.VMEM((pairs, rows, LANES), bf16),
            pltpu.VMEM((2 * pairs * ELEM_NODES, LANES), f32),
            pltpu.VMEM((n, pairs * 12, lanes), bf16),
            pltpu.VMEM((pairs * 12, lanes), f32),
            pltpu.VMEM((max(n, 4), 8 * pad, LANES), f32),
            pltpu.VMEM((16 * low, width), f32),
            pltpu.VMEM((n, segs, lanes), bf16),
            pltpu.VMEM((n, segs, lanes), bf16),
            pltpu.VMEM((n, segs, lanes), bf16),
            pltpu.VMEM(packed, bf16),
            pltpu.VMEM(packed, bf16),
            pltpu.VMEM((1, ns, LANES, lanes), bf16),
            pltpu.VMEM((1, ns, LANES, lanes), bf16),
            pltpu.VMEM((n, 8 * pad, LANES), f32),
            pltpu.VMEM((n, 8 * pad, LANES), f32),
            pltpu.VMEM((16, 16, width), f32),
            pltpu.VMEM((n * pairs, pad, LANES), f32),
            sems(n), sems(ns), sems(n), sems(ns), sems(n), sems(n, groups // 8), sems(n), sems(ns),
        ),
        compiler_params=pltpu.CompilerParams(collective_id=0, has_side_effects=True, vmem_limit_bytes=VMEM_LIMIT),
        cost_estimate=pl.CostEstimate(flops=4 * modes * rows * rows * nodes, bytes_accessed=8 << 20, transcendentals=0),
    )(
        field, stiffness, kl_coef, triple_mode, triple_row, triple_col, triple_value, die_elem, die_side, seg_owner,
        seg_face, die_mortar, int_mortar, bump_coef.T, int_elem, int_side, sel, sel.T,
    )


def solution(mesh):
    in_specs = (
        P("chaos", "space"),
        P(("space", "chaos"), None),
        P(None, ("space", "chaos")),
        P(),
        P(),
        P(),
        P(),
        P(("space", "chaos")),
        P(("space", "chaos")),
        P(("space", "chaos")),
        P(("space", "chaos")),
        P(("space", "chaos"), None),
        P(("space", "chaos"), None),
        P(("space", "chaos"), None),
        P(("space", "chaos")),
        P(("space", "chaos")),
    )
    out_specs = P("chaos", "space")
    return jax.shard_map(local, mesh=mesh, in_specs=in_specs, out_specs=out_specs, check_vma=False)
```
